32 devices in a mesh: heads: 4 (over x, core), cells: 8 (over z, y).
Axes of the slice: x: 2, y: 2, z: 4, core: 2. Of those that a mesh axis runs over, the one named last changes fastest.
Arguments:
- cells_in: bfloat16 [8, 1024, 1024], P(None, ('heads', 'cells')), may hold values from -6 to 6
- gain: float32 [1024], replicated, may hold values from 0.1 to 1.9
- w_qkv: bfloat16 [1024, 3072], replicated
- w_out: bfloat16 [1024, 1024], replicated, may hold values from -0.1875 to 0.1875
- tile_of_cell: int32 [1024], P(('heads', 'cells')), may hold values from 0 to 255
- tile_adjacent: int32 [256, 256], replicated, may hold values from 0 to 1, as said below
Outputs:
- cells_out: bfloat16 [8, 1024, 1024], P(None, ('heads', 'cells'))
The draws below stay inside these ranges and needn't reach their ends.
Inputs may be any that keep to these rules, and one draw needn't show every extreme that they name: Tiles sit at the places of a 16 x 16 grid in an order drawn from the seed; tile_adjacent is 1 exactly where the two tiles' places differ by at most one in each grid direction, so it is symmetric with ones on the diagonal.
All inputs are finite; a program needn't handle non-finite values.
Results may differ from the reference program's by a relative error of at most 0.011.
Values may be sent and summed in bfloat16 or wider, within the bound.
No kernel may reach another device: no remote copies, remote signals or barrier semaphores. Data moves between devices by JAX's collectives and lax.ppermute only.
A program may use at most 64 MiB of HBM per device.

```python
import math
import jax
import jax.numpy as jnp
from jax import lax

GENES = 8
HEADS = 16
HEAD_DIM = 64
D = 1024
CELLS = 1024
TSIDE = 16
TILES = 256


def draw_w_qkv(key, part):
    key_matrix = jax.random.split(jax.random.fold_in(key, 11), 3)
    w_query = jax.random.normal(key_matrix[0], (D, D), jnp.float32) * (2.0 / math.sqrt(D))
    w_key = jax.random.normal(key_matrix[1], (D, D), jnp.float32) * (1.0 / math.sqrt(D))
    w_value = jax.random.normal(key_matrix[2], (D, D), jnp.float32) * (1.0 / math.sqrt(D))
    return jnp.concatenate([w_query, w_key, w_value], axis=1).astype(jnp.bfloat16)


def draw_tile_adjacent(key, part):
    places = jax.random.permutation(jax.random.fold_in(key, 23), TILES)
    row_location = places // TSIDE
    col_pos = places % TSIDE
    near_rows = jnp.abs(row_location[:, None] - row_location[None, :]) <= 1
    neighbour_columns = jnp.abs(col_pos[:, None] - col_pos[None, :]) <= 1
    return (near_rows & neighbour_columns).astype(jnp.int32)


def touch_ends(result, key, low, largest):
    dims = result.shape
    place = [jax.random.randint(jax.random.fold_in(key, axis), (), 0, dims[axis]) for axis in range(len(dims))]
    result = result.at[tuple(place)].set(low)
    longest = dims.index(max(dims))
    place[longest] = (place[longest] + 1) % dims[longest]
    return result.at[tuple(place)].set(largest)


def block_scale(rng, extent, cuts, smallest, high):
    factor_of = 1.0
    for position, parts in cuts:
        draws = jax.random.uniform(jax.random.fold_in(jax.random.fold_in(rng, 6), position), (parts,), jnp.float32, smallest / len(cuts), high / len(cuts))
        factor_of = factor_of * jnp.repeat(jnp.exp(draws), extent[position] // parts).reshape((-1,) + (1,) * (len(extent) - 1 - position))
    return factor_of


def bell_draw(key, extent, scale, reach, shards=(), kind=jnp.bfloat16):
    entries = scale * jax.random.normal(key, extent, jnp.float32)
    if shards:
        entries = entries * block_scale(key, extent, shards, -0.22, 0.18)
    return jnp.clip(entries, -reach, reach).astype(kind)


def setup_inputs(seed: int = 0) -> dict:
    seeds = jax.random.split(jax.random.key(seed), 7)
    cells_in = bell_draw(seeds[0], (GENES, CELLS, D), 1.0, 6.0, ((1, 32),))
    gain = jnp.clip(1.0 + 0.18 * jax.random.normal(seeds[1], (D,), jnp.float32), 0.1, 1.9)
    w_qkv = draw_w_qkv(jax.random.fold_in(seeds[6], 71), 0)
    w_out = bell_draw(seeds[3], (D, D), D ** -0.5, 0.1875)
    tile_of_cell = touch_ends(jax.random.randint(seeds[4], (CELLS,), 0, TILES), jax.random.fold_in(seeds[4], 1), 0, TILES - 1).astype(jnp.int32)
    tile_adjacent = draw_tile_adjacent(jax.random.fold_in(seeds[6], 71), 0)
    return dict(cells_in=cells_in, gain=gain, w_qkv=w_qkv, w_out=w_out, tile_of_cell=tile_of_cell, tile_adjacent=tile_adjacent)


def attend_item(item, allowed):
    query_matrix, key_matrix, value_matrix = item
    logit_scores = jnp.dot(query_matrix, key_matrix.T, preferred_element_type=jnp.float32) * 0.125
    masked = jnp.where(allowed, logit_scores, -1e+30)
    top = lax.optimization_barrier(jnp.max(masked, axis=-1))
    softmax_weights = jnp.where(allowed, jnp.exp(masked - top[:, None]), 0.0)
    total = lax.optimization_barrier(jnp.sum(softmax_weights, axis=-1))
    summed = jnp.dot(softmax_weights.astype(jnp.bfloat16), value_matrix, preferred_element_type=jnp.float32)
    return (summed / total[:, None]).astype(jnp.bfloat16)

def reference(cells_in, gain, w_qkv, w_out, tile_of_cell, tile_adjacent):
    x32 = cells_in.astype(jnp.float32)
    normed = (x32 * lax.rsqrt(lax.optimization_barrier(jnp.mean(x32 * x32, axis=-1, keepdims=True)) + 1e-05) * gain).astype(jnp.bfloat16)
    qkv = jnp.dot(normed.reshape(GENES * CELLS, D), w_qkv, preferred_element_type=jnp.float32).astype(jnp.bfloat16)
    qkv = qkv.reshape(GENES, CELLS, 3, HEADS, HEAD_DIM).transpose(2, 0, 3, 1, 4).reshape(3, GENES * HEADS, CELLS, HEAD_DIM)
    allowed = tile_adjacent[tile_of_cell[:, None], tile_of_cell[None, :]].astype(jnp.int32)
    is_allowed = allowed > 0
    attended = lax.map(lambda item: attend_item(item, is_allowed), (qkv[0], qkv[1], qkv[2]))
    attended = attended.reshape(GENES, HEADS, CELLS, HEAD_DIM).transpose(0, 2, 1, 3).reshape(GENES * CELLS, D)
    attention_output = jnp.dot(attended, w_out, preferred_element_type=jnp.float32).astype(jnp.bfloat16)
    return attention_output.reshape(GENES, CELLS, D)
```

```python
import functools
import math

import jax
import jax.numpy as jnp
from jax import lax
from jax.experimental import pallas as pl
from jax.experimental.pallas import tpu as pltpu
from jax.sharding import PartitionSpec as P

HEAD_DIM = 64
PAIR = 2 * HEAD_DIM
VAL_ROWS = HEAD_DIM + 16
ACC_ROWS = HEAD_DIM + 8
MASKED = -1e30
SCALE = 0.125 * math.log2(math.e)
BLOCK = 512


def normalise(rows, gain):
    x32 = rows.astype(jnp.float32)
    mean = jnp.mean(x32 * x32, axis=-1, keepdims=True)
    return (x32 * lax.rsqrt(mean + 1e-05) * gain).astype(jnp.bfloat16)


def dot(a, b, a_dim=1, b_dim=0):
    return lax.dot_general(
        a, b, (((a_dim,), (b_dim,)), ((), ())), preferred_element_type=jnp.float32
    )


def one_hot(tiles, count):
    places = lax.broadcasted_iota(jnp.int32, (count, tiles.shape[1]), 0)
    return (places == tiles).astype(jnp.float32).astype(jnp.bfloat16)


def query_rows(adj_ref, tiles):
    adjacency = adj_ref[...].astype(jnp.float32).astype(jnp.bfloat16)
    return dot(adjacency, one_hot(tiles, adjacency.shape[0])).astype(jnp.bfloat16)


def absorb_block(rows, tiles, near, gain, wk_ref, wvt_ref, query_ref, acc_ref, top_ref, key_ref, val_ref, bias_ref, first):
    width = rows.shape[1]
    heads = width // HEAD_DIM
    normed = normalise(rows, gain)
    for start in range(0, width, 256):
        key_ref[:, start : start + 256] = dot(normed, wk_ref[:, start : start + 256]).astype(
            jnp.bfloat16
        )
    for start in range(0, width, 256):
        values = dot(wvt_ref[start : start + 256, :], normed, 1, 1).astype(jnp.bfloat16)
        for part in range(256 // HEAD_DIM):
            head = start // HEAD_DIM + part
            val_ref[head, :HEAD_DIM, :] = values[part * HEAD_DIM : (part + 1) * HEAD_DIM]
    allowed = dot(one_hot(tiles, near.shape[0]), near, 0, 0)
    bias_ref[...] = (allowed - 1.0) * -MASKED
    for head in range(heads):
        pair = slice(head // 2 * PAIR, head // 2 * PAIR + PAIR)
        query = query_ref[:, pair]
        lane = lax.broadcasted_iota(jnp.int32, query.shape, 1)
        query = jnp.where((lane // HEAD_DIM) == head % 2, query, jnp.zeros_like(query))
        scores = dot(key_ref[:, pair], query, 1, 1) + bias_ref[...]
        top = jnp.max(scores, axis=0, keepdims=True)
        if not first:
            before = top_ref[head : head + 1, :]
            top = jnp.maximum(top, before)
        weights = jnp.exp2(scores - top).astype(jnp.bfloat16)
        summed = dot(val_ref[head], weights)[:ACC_ROWS]
        if not first:
            summed = summed + acc_ref[head] * jnp.exp2(before - top)
        acc_ref[head] = summed
        top_ref[head : head + 1, :] = top


def absorb_all(chunks, tile_refs, near, gain, wk_ref, wvt_ref, query_ref, acc_ref, top_ref, key_ref, val_ref, bias_ref, first):
    block = key_ref.shape[0]
    for chunk, tile_ref in zip(chunks, tile_refs):
        for start in range(0, chunk.shape[0], block):
            absorb_block(
                chunk[start : start + block, :],
                tile_ref[:, start : start + block],
                near,
                gain,
                wk_ref,
                wvt_ref,
                query_ref,
                acc_ref,
                top_ref,
                key_ref,
                val_ref,
                bias_ref,
                first,
            )
            first = False


def set_ones(val_ref):
    heads, _, block = val_ref.shape
    val_ref[:, HEAD_DIM:, :] = jnp.ones((heads, VAL_ROWS - HEAD_DIM, block), jnp.bfloat16)


def first_kernel(count, xq_ref, tq_ref, gain_ref, adj_ref, wq_ref, wk_ref, wvt_ref, *refs):
    chunks, tile_refs, rest = refs[:count], refs[count : 2 * count], refs[2 * count :]
    query_ref, acc_ref, top_ref, key_ref, val_ref, bias_ref = rest
    gain = gain_ref[...]
    width = xq_ref.shape[1]
    set_ones(val_ref)
    normed = normalise(xq_ref[...], gain)
    for start in range(0, width, 256):
        part = dot(normed, wq_ref[:, start : start + 256]) * SCALE
        query_ref[:, start : start + 256] = part.astype(jnp.bfloat16)
    near = query_rows(adj_ref, tq_ref[...])
    absorb_all(chunks, tile_refs, near, gain, wk_ref, wvt_ref, query_ref, acc_ref, top_ref, key_ref, val_ref, bias_ref, True)


def last_kernel(count, query_ref, acc_in, top_in, tq_ref, gain_ref, adj_ref, wk_ref, wvt_ref, wo_ref, *refs):
    chunks, tile_refs, rest = refs[:count], refs[count : 2 * count], refs[2 * count :]
    out_ref, acc_ref, top_ref, key_ref, val_ref, bias_ref, att_ref = rest
    set_ones(val_ref)
    acc_ref[...] = acc_in[...]
    top_ref[...] = top_in[...]
    near = query_rows(adj_ref, tq_ref[...])
    absorb_all(
        chunks, tile_refs, near, gain_ref[...], wk_ref, wvt_ref, query_ref, acc_ref, top_ref, key_ref, val_ref, bias_ref, False
    )
    for head in range(acc_ref.shape[0]):
        total = acc_ref[head, HEAD_DIM : HEAD_DIM + 1, :]
        part = acc_ref[head, :HEAD_DIM, :] / total
        att_ref[head * HEAD_DIM : (head + 1) * HEAD_DIM, :] = part.astype(jnp.bfloat16)
    attended = att_ref[...]
    width = attended.shape[0]
    for start in range(0, width, 256):
        out_ref[:, start : start + 256] = dot(attended, wo_ref[:, start : start + 256], 0, 0).astype(
            jnp.bfloat16
        )


def vmem(count):
    return [pl.BlockSpec(memory_space=pltpu.VMEM)] * count


def scratch(block, queries, heads):
    return [
        pltpu.VMEM((block, heads * HEAD_DIM), jnp.bfloat16),
        pltpu.VMEM((heads, VAL_ROWS, block), jnp.bfloat16),
        pltpu.VMEM((block, queries), jnp.float32),
    ]


PARAMS = pltpu.CompilerParams(vmem_limit_bytes=48 * 1024 * 1024)


def call_first(xq, tq, gain, adjacency, wq, wk, wvt, chunks, tiles):
    queries, width = xq.shape
    heads = width // HEAD_DIM
    block = math.gcd(BLOCK, chunks[0].shape[0])
    operands = (xq, tq, gain, adjacency, wq, wk, wvt, *chunks, *tiles)
    return pl.pallas_call(
        functools.partial(first_kernel, len(chunks)),
        out_shape=(
            jax.ShapeDtypeStruct((queries, width), jnp.bfloat16),
            jax.ShapeDtypeStruct((heads, ACC_ROWS, queries), jnp.float32),
            jax.ShapeDtypeStruct((heads, queries), jnp.float32),
        ),
        in_specs=vmem(len(operands)),
        out_specs=tuple(vmem(3)),
        scratch_shapes=scratch(block, queries, heads),
        compiler_params=PARAMS,
        name="attend_first",
    )(*operands)


def call_last(query, acc, top, tq, gain, adjacency, wk, wvt, wo, chunks, tiles):
    queries, width = query.shape
    heads = width // HEAD_DIM
    block = math.gcd(BLOCK, chunks[0].shape[0])
    operands = (query, acc, top, tq, gain, adjacency, wk, wvt, wo, *chunks, *tiles)
    return pl.pallas_call(
        functools.partial(last_kernel, len(chunks)),
        out_shape=jax.ShapeDtypeStruct((queries, width), jnp.bfloat16),
        in_specs=vmem(len(operands)),
        out_specs=vmem(1)[0],
        scratch_shapes=[
            pltpu.VMEM((heads, ACC_ROWS, queries), jnp.float32),
            pltpu.VMEM((heads, queries), jnp.float32),
            *scratch(block, queries, heads),
            pltpu.VMEM((width, queries), jnp.bfloat16),
        ],
        compiler_params=PARAMS,
        name="attend_last",
    )(*operands)


def on_device(cells_in, gain, w_qkv, w_out, tile_of_cell, tile_adjacent):
    genes, cell_dev, width = cells_in.shape
    head_devs, cell_devs = lax.axis_size("heads"), lax.axis_size("cells")
    sets = cell_devs // genes
    across = [[s * genes + g for g in range(genes)] for s in range(sets)]
    same = [[s * genes + g for s in range(sets)] for g in range(genes)]

    def partner(value, step):
        return lax.ppermute(value, "heads", [(i, i ^ step) for i in range(head_devs)])

    own = lax.all_to_all(cells_in, "cells", 0, 0, axis_index_groups=across, tiled=True)
    own = own.reshape(genes * cell_dev, width)
    spread = jnp.broadcast_to(tile_of_cell[None], (genes, cell_dev))
    tile_own = lax.all_to_all(spread, "cells", 0, 0, axis_index_groups=across, tiled=True)
    tile_own = tile_own.reshape(1, genes * cell_dev)
    held, tile_held = own, tile_own
    if sets > 1:
        held = lax.all_gather(own, "cells", axis=0, axis_index_groups=same, tiled=True)
        tile_held = lax.all_gather(tile_own, "cells", axis=1, axis_index_groups=same, tiled=True)
    chunks, tiles = [held], [tile_held]
    for step in range(2, head_devs, 2):
        chunks.append(partner(held, step))
        tiles.append(partner(tile_held, step))
    beside = [partner(chunk, 1) for chunk in chunks]
    tiles_beside = [partner(tile, 1) for tile in tiles]

    gain = gain.reshape(1, width)
    wq, wk, wvt = w_qkv[:, :width], w_qkv[:, width : 2 * width], w_qkv[:, 2 * width :].T
    query, acc, top = call_first(
        own, tile_own, gain, tile_adjacent, wq, wk, wvt, [chunks[0], beside[0]], [tiles[0], tiles_beside[0]]
    )
    out = call_last(
        query, acc, top, tile_own, gain, tile_adjacent, wk, wvt, w_out,
        [*chunks[1:], *beside[1:]], [*tiles[1:], *tiles_beside[1:]],
    )
    out = out.reshape(genes, cell_dev, width)
    return lax.all_to_all(out, "cells", 0, 0, axis_index_groups=across, tiled=True)


def solution(mesh):
    return jax.shard_map(
        on_device,
        mesh=mesh,
        in_specs=(P(None, ("heads", "cells"), None), P(), P(), P(), P(("heads", "cells")), P()),
        out_specs=P(None, ("heads", "cells"), None),
        check_vma=False,
    )
```

```python
import functools
import math

import jax
import jax.numpy as jnp
from jax import lax
from jax.experimental import pallas as pl
from jax.experimental.pallas import tpu as pltpu
from jax.sharding import PartitionSpec as P

HEAD_DIM = 64
PAIR = 2 * HEAD_DIM
VAL_ROWS = HEAD_DIM + 16
ACC_ROWS = HEAD_DIM + 8
MASKED = -1e30
SCALE = 0.125 * math.log2(math.e)
BLOCK = 256
COLS = 256


def normalise(rows, gain):
    x32 = rows.astype(jnp.float32)
    mean = jnp.mean(x32 * x32, axis=-1, keepdims=True)
    return (x32 * lax.rsqrt(mean + 1e-05) * gain).astype(jnp.bfloat16)


def dot(a, b, a_dim=1, b_dim=0):
    return lax.dot_general(
        a, b, (((a_dim,), (b_dim,)), ((), ())), preferred_element_type=jnp.float32
    )


def one_hot(tiles, count):
    places = lax.broadcasted_iota(jnp.int32, (count, tiles.shape[1]), 0)
    return (places == tiles).astype(jnp.float32).astype(jnp.bfloat16)


def query_rows(adj_ref, tiles):
    adjacency = adj_ref[...].astype(jnp.float32).astype(jnp.bfloat16)
    return dot(adjacency, one_hot(tiles, adjacency.shape[0])).astype(jnp.bfloat16)


class Work:
    def __init__(self, gain, w_ref, near, query_ref, acc_ref, top_ref, scratch):
        self.gain, self.w_ref, self.near = gain, w_ref, near
        self.query_ref, self.acc_ref, self.top_ref = query_ref, acc_ref, top_ref
        self.norm_ref, self.key_ref, self.val_ref, self.bias_ref, self.weight_ref = scratch
        heads, _, block = self.val_ref.shape
        ones = jnp.ones((heads, VAL_ROWS - HEAD_DIM, block), jnp.bfloat16)
        self.val_ref[:, HEAD_DIM:, :] = ones

    def normal(self, pieces):
        start = 0
        for piece in pieces:
            self.norm_ref[start : start + piece.shape[0], :] = normalise(piece, self.gain)
            start += piece.shape[0]
        return self.norm_ref[...]

    def project_queries(self, pieces):
        normed = self.normal(pieces)
        for start in range(0, normed.shape[1], COLS):
            part = dot(normed, self.w_ref[:, start : start + COLS]) * SCALE
            self.query_ref[:, start : start + COLS] = part.astype(jnp.bfloat16)

    def absorb(self, pieces, tiles, first):
        normed = self.normal(pieces)
        width = normed.shape[1]
        heads = width // HEAD_DIM
        for start in range(0, width, COLS):
            keys = dot(normed, self.w_ref[:, width + start : width + start + COLS])
            self.key_ref[:, start : start + COLS] = keys.astype(jnp.bfloat16)
        allowed = dot(one_hot(tiles, self.near.shape[0]), self.near, 0, 0)
        self.bias_ref[...] = (allowed - 1.0) * -MASKED
        for start in range(0, width, COLS):
            values = dot(normed, self.w_ref[:, 2 * width + start : 2 * width + start + COLS])
            values = values.astype(jnp.bfloat16).T
            for part in range(COLS // HEAD_DIM):
                rows = slice(part * HEAD_DIM, (part + 1) * HEAD_DIM)
                self.val_ref[start // HEAD_DIM + part, :HEAD_DIM, :] = values[rows]
        factors = []
        for head in range(heads):
            pair = slice(head // 2 * PAIR, head // 2 * PAIR + PAIR)
            query = self.query_ref[:, pair]
            lane = lax.broadcasted_iota(jnp.int32, query.shape, 1)
            query = jnp.where((lane // HEAD_DIM) == head % 2, query, jnp.zeros_like(query))
            scores = dot(self.key_ref[:, pair], query, 1, 1) + self.bias_ref[...]
            top = jnp.max(scores, axis=0, keepdims=True)
            if not first:
                before = self.top_ref[head : head + 1, :]
                top = jnp.maximum(top, before)
                factors.append(jnp.exp2(before - top))
            self.weight_ref[head] = jnp.exp2(scores - top).astype(jnp.bfloat16)
            self.top_ref[head : head + 1, :] = top
        for head in range(heads):
            summed = dot(self.val_ref[head], self.weight_ref[head])[:ACC_ROWS]
            if not first:
                summed = summed + self.acc_ref[head] * factors[head]
            self.acc_ref[head] = summed


def blocks_of(chunks, tile_refs, block):
    held = []
    for chunk, tile_ref in zip(chunks, tile_refs):
        step = min(block, chunk.shape[0])
        for start in range(0, chunk.shape[0], step):
            held.append((chunk[start : start + step, :], tile_ref[:, start : start + step]))
    per = block // held[0][0].shape[0]
    for start in range(0, len(held), per):
        group = held[start : start + per]
        yield [rows for rows, _ in group], jnp.concatenate([tiles for _, tiles in group], axis=1)


def first_kernel(queries, count, tq_ref, gain_ref, adj_ref, w_ref, *refs):
    query_x, refs = refs[:queries], refs[queries:]
    chunks, tile_refs, rest = refs[:count], refs[count : 2 * count], refs[2 * count :]
    query_ref, acc_ref, top_ref, *scratch = rest
    near = query_rows(adj_ref, tq_ref[...])
    work = Work(gain_ref[...], w_ref, near, query_ref, acc_ref, top_ref, scratch)
    work.project_queries([ref[...] for ref in query_x])
    first = True
    for pieces, tiles in blocks_of(chunks, tile_refs, scratch[0].shape[0]):
        work.absorb(pieces, tiles, first)
        first = False


def next_kernel(count, query_ref, acc_in, top_in, tq_ref, gain_ref, adj_ref, w_ref, *refs):
    chunks, tile_refs, rest = refs[:count], refs[count : 2 * count], refs[2 * count :]
    acc_ref, top_ref, *scratch = rest
    near = query_rows(adj_ref, tq_ref[...])
    acc_ref[...] = acc_in[...]
    top_ref[...] = top_in[...]
    work = Work(gain_ref[...], w_ref, near, query_ref, acc_ref, top_ref, scratch)
    for pieces, tiles in blocks_of(chunks, tile_refs, scratch[0].shape[0]):
        work.absorb(pieces, tiles, False)


def last_kernel(count, query_ref, acc_in, top_in, tq_ref, gain_ref, adj_ref, w_ref, wo_ref, *refs):
    chunks, tile_refs, rest = refs[:count], refs[count : 2 * count], refs[2 * count :]
    out_ref, acc_ref, top_ref, att_ref, *scratch = rest
    near = query_rows(adj_ref, tq_ref[...])
    acc_ref[...] = acc_in[...]
    top_ref[...] = top_in[...]
    work = Work(gain_ref[...], w_ref, near, query_ref, acc_ref, top_ref, scratch)
    for pieces, tiles in blocks_of(chunks, tile_refs, scratch[0].shape[0]):
        work.absorb(pieces, tiles, False)
    for head in range(acc_ref.shape[0]):
        total = acc_ref[head, HEAD_DIM : HEAD_DIM + 1, :]
        part = acc_ref[head, :HEAD_DIM, :] / total
        att_ref[head * HEAD_DIM : (head + 1) * HEAD_DIM, :] = part.astype(jnp.bfloat16)
    attended = att_ref[...].T
    for start in range(0, attended.shape[1], COLS):
        out = dot(attended, wo_ref[:, start : start + COLS])
        out_ref[:, start : start + COLS] = out.astype(jnp.bfloat16)


def vmem(count):
    return [pl.BlockSpec(memory_space=pltpu.VMEM)] * count


def scratch(queries, heads):
    return [
        pltpu.VMEM((BLOCK, heads * HEAD_DIM), jnp.bfloat16),
        pltpu.VMEM((BLOCK, heads * HEAD_DIM), jnp.bfloat16),
        pltpu.VMEM((heads, VAL_ROWS, BLOCK), jnp.bfloat16),
        pltpu.VMEM((BLOCK, queries), jnp.float32),
        pltpu.VMEM((heads, BLOCK, queries), jnp.bfloat16),
    ]


def cost(queries, keys, width, more):
    flops = 2 * (2 * keys * width * width + 4 * queries * keys * width + more * queries * width * width)
    return pl.CostEstimate(flops=flops, bytes_accessed=8 * width * width, transcendentals=0)


PARAMS = pltpu.CompilerParams(vmem_limit_bytes=32 * 1024 * 1024)


def state_shapes(heads, queries):
    return (
        jax.ShapeDtypeStruct((heads, ACC_ROWS, queries), jnp.float32),
        jax.ShapeDtypeStruct((heads, queries), jnp.float32),
    )


def call_first(query_x, tq, gain, adjacency, w_qkv, chunks, tiles):
    queries, width = tq.shape[1], w_qkv.shape[0]
    heads = width // HEAD_DIM
    operands = (tq, gain, adjacency, w_qkv, *query_x, *chunks, *tiles)
    return pl.pallas_call(
        functools.partial(first_kernel, len(query_x), len(chunks)),
        out_shape=(jax.ShapeDtypeStruct((queries, width), jnp.bfloat16), *state_shapes(heads, queries)),
        in_specs=vmem(len(operands)),
        out_specs=tuple(vmem(3)),
        scratch_shapes=scratch(queries, heads),
        compiler_params=PARAMS,
        cost_estimate=cost(queries, sum(c.shape[0] for c in chunks), width, 1),
        name="attend_first",
    )(*operands)


def call_next(query, acc, top, tq, gain, adjacency, w_qkv, chunks, tiles):
    queries, width = query.shape
    heads = width // HEAD_DIM
    operands = (query, acc, top, tq, gain, adjacency, w_qkv, *chunks, *tiles)
    return pl.pallas_call(
        functools.partial(next_kernel, len(chunks)),
        out_shape=state_shapes(heads, queries),
        in_specs=vmem(len(operands)),
        out_specs=tuple(vmem(2)),
        scratch_shapes=scratch(queries, heads),
        compiler_params=PARAMS,
        cost_estimate=cost(queries, sum(c.shape[0] for c in chunks), width, 0),
        name="attend_next",
    )(*operands)


def call_last(query, acc, top, tq, gain, adjacency, w_qkv, wo, chunks, tiles):
    queries, width = query.shape
    heads = width // HEAD_DIM
    operands = (query, acc, top, tq, gain, adjacency, w_qkv, wo, *chunks, *tiles)
    return pl.pallas_call(
        functools.partial(last_kernel, len(chunks)),
        out_shape=jax.ShapeDtypeStruct((queries, width), jnp.bfloat16),
        in_specs=vmem(len(operands)),
        out_specs=vmem(1)[0],
        scratch_shapes=[
            pltpu.VMEM((heads, ACC_ROWS, queries), jnp.float32),
            pltpu.VMEM((heads, queries), jnp.float32),
            pltpu.VMEM((width, queries), jnp.bfloat16),
            *scratch(queries, heads),
        ],
        compiler_params=PARAMS,
        cost_estimate=cost(queries, sum(c.shape[0] for c in chunks), width, 1),
        name="attend_last",
    )(*operands)


def on_device(cells_in, gain, w_qkv, w_out, tile_of_cell, tile_adjacent):
    genes, cell_dev, width = cells_in.shape
    head_devs, cell_devs = lax.axis_size("heads"), lax.axis_size("cells")
    sets = cell_devs // genes
    half = genes // 2
    gene = lax.rem(lax.axis_index("cells"), genes)
    same = [[s * genes + g for s in range(sets)] for g in range(genes)]

    def over_cells(value, step):
        return lax.ppermute(value, "cells", [(i, i ^ step) for i in range(cell_devs)])

    def over_heads(value, step):
        return lax.ppermute(value, "heads", [(i, i ^ step) for i in range(head_devs)])

    def gather_sets(value, axis):
        if sets == 1:
            return value
        return lax.all_gather(value, "cells", axis=axis, axis_index_groups=same, tiled=True)

    pieces = [lax.dynamic_index_in_dim(cells_in, gene ^ k, 0, keepdims=False) for k in range(genes)]
    tile_own = tile_of_cell.reshape(1, cell_dev)
    step = 1
    while step < genes:
        tile_own = jnp.concatenate([tile_own, over_cells(tile_own, step)], axis=1)
        step *= 2
    arrived = [pieces[0]] + [None] * (genes - 1)
    for k in [*range(half, genes), *range(1, half)]:
        arrived[k] = over_cells(pieces[k], k)
    parts = [jnp.concatenate(arrived[:half], 0), jnp.concatenate(arrived[half:], 0)]
    tile_parts = [tile_own[:, : half * cell_dev], tile_own[:, half * cell_dev :]]
    chunks = [[], []]
    tiles = [[], []]
    for i in range(2):
        held, tile_held = gather_sets(parts[i], 0), gather_sets(tile_parts[i], 1)
        for step in range(0, head_devs, 2):
            chunk = held if step == 0 else over_heads(held, step)
            tile = tile_held if step == 0 else over_heads(tile_held, step)
            chunks[i] += [chunk, over_heads(chunk, 1)]
            tiles[i] += [tile, over_heads(tile, 1)]
    gain = gain.reshape(1, width)
    query, acc, top = call_first(
        parts, tile_own, gain, tile_adjacent, w_qkv, chunks[0][:2] + chunks[1][:2], tiles[0][:2] + tiles[1][:2]
    )
    acc, top = call_next(query, acc, top, tile_own, gain, tile_adjacent, w_qkv, chunks[0][2:], tiles[0][2:])
    out = call_last(
        query, acc, top, tile_own, gain, tile_adjacent, w_qkv, w_out, chunks[1][2:], tiles[1][2:]
    )
    out = out.reshape(genes, cell_dev, width)
    result = jnp.zeros_like(out)
    for k in [*range(half, genes), *range(1, half), 0]:
        piece = out[k] if k == 0 else over_cells(out[k], k)
        result = lax.dynamic_update_index_in_dim(result, piece, gene ^ k, 0)
    return result


def solution(mesh):
    return jax.shard_map(
        on_device,
        mesh=mesh,
        in_specs=(P(None, ("heads", "cells"), None), P(), P(), P(), P(("heads", "cells")), P()),
        out_specs=P(None, ("heads", "cells"), None),
        check_vma=False,
    )
```

```python
import functools
import math

import jax
import jax.numpy as jnp
from jax import lax
from jax.experimental import pallas as pl
from jax.experimental.pallas import tpu as pltpu
from jax.sharding import PartitionSpec as P

HEAD_DIM = 64
PAIR = 2 * HEAD_DIM
VAL_ROWS = HEAD_DIM + 16
ACC_ROWS = HEAD_DIM + 8
MASKED = -1e30
SCALE = 0.125 * math.log2(math.e)
BLOCK = 256
COLS = 256
TAG = 128


def normalise(rows, gain):
    x32 = rows.astype(jnp.float32)
    mean = jnp.mean(x32 * x32, axis=-1, keepdims=True)
    return (x32 * lax.rsqrt(mean + 1e-05) * gain).astype(jnp.bfloat16)


def dot(a, b, a_dim=1, b_dim=0):
    return lax.dot_general(
        a, b, (((a_dim,), (b_dim,)), ((), ())), preferred_element_type=jnp.float32
    )


def one_hot(pieces, width, count):
    tags = jnp.concatenate([piece[:, width:] for piece in pieces], axis=0).astype(jnp.float32)
    lane = lax.broadcasted_iota(jnp.int32, tags.shape, 1).astype(jnp.float32)
    parts = [(tags == lane + start).astype(jnp.float32) for start in range(0, count, TAG)]
    return jnp.concatenate(parts, axis=1).astype(jnp.bfloat16)


def query_rows(adj_ref, pieces, width):
    adjacency = adj_ref[...].astype(jnp.float32).astype(jnp.bfloat16)
    return dot(adjacency, one_hot(pieces, width, adjacency.shape[0]), 1, 1).astype(jnp.bfloat16)


class Work:
    def __init__(self, gain, w_ref, near, query_ref, acc_ref, top_ref, scratch):
        self.gain, self.w_ref, self.near = gain, w_ref, near
        self.query_ref, self.acc_ref, self.top_ref = query_ref, acc_ref, top_ref
        self.norm_ref, self.key_ref, self.val_ref, self.bias_ref, self.weight_ref = scratch
        heads, _, block = self.val_ref.shape
        ones = jnp.ones((heads, VAL_ROWS - HEAD_DIM, block), jnp.bfloat16)
        self.val_ref[:, HEAD_DIM:, :] = ones

    def normal(self, pieces):
        start = 0
        for piece in pieces:
            self.norm_ref[start : start + piece.shape[0], :] = normalise(piece[:, : self.gain.shape[1]], self.gain)
            start += piece.shape[0]
        return self.norm_ref[...]

    def project_queries(self, pieces):
        normed = self.normal(pieces)
        for start in range(0, normed.shape[1], COLS):
            part = dot(normed, self.w_ref[:, start : start + COLS]) * SCALE
            self.query_ref[:, start : start + COLS] = part.astype(jnp.bfloat16)

    def absorb(self, pieces, first):
        normed = self.normal(pieces)
        width = normed.shape[1]
        heads = width // HEAD_DIM
        for start in range(0, width, COLS):
            keys = dot(normed, self.w_ref[:, width + start : width + start + COLS])
            self.key_ref[:, start : start + COLS] = keys.astype(jnp.bfloat16)
        allowed = dot(one_hot(pieces, width, self.near.shape[0]), self.near)
        self.bias_ref[...] = (allowed - 1.0) * -MASKED
        for start in range(0, width, COLS):
            values = dot(normed, self.w_ref[:, 2 * width + start : 2 * width + start + COLS])
            values = values.astype(jnp.bfloat16).T
            for part in range(COLS // HEAD_DIM):
                rows = slice(part * HEAD_DIM, (part + 1) * HEAD_DIM)
                self.val_ref[start // HEAD_DIM + part, :HEAD_DIM, :] = values[rows]
        factors = []
        for head in range(heads):
            pair = slice(head // 2 * PAIR, head // 2 * PAIR + PAIR)
            query = self.query_ref[:, pair]
            lane = lax.broadcasted_iota(jnp.int32, query.shape, 1)
            query = jnp.where((lane // HEAD_DIM) == head % 2, query, jnp.zeros_like(query))
            scores = dot(self.key_ref[:, pair], query, 1, 1) + self.bias_ref[...]
            top = jnp.max(scores, axis=0, keepdims=True)
            if not first:
                before = self.top_ref[head : head + 1, :]
                top = jnp.maximum(top, before)
                factors.append(jnp.exp2(before - top))
            self.weight_ref[head] = jnp.exp2(scores - top).astype(jnp.bfloat16)
            self.top_ref[head : head + 1, :] = top
        for head in range(heads):
            summed = dot(self.val_ref[head], self.weight_ref[head])[:ACC_ROWS]
            if not first:
                summed = summed + self.acc_ref[head] * factors[head]
            self.acc_ref[head] = summed


def blocks_of(chunks, block):
    held = []
    for chunk in chunks:
        step = min(block, chunk.shape[0])
        held += [chunk[start : start + step, :] for start in range(0, chunk.shape[0], step)]
    per = block // held[0].shape[0]
    for start in range(0, len(held), per):
        yield held[start : start + per]


def first_kernel(queries, gain_ref, adj_ref, w_ref, *refs):
    count = len(refs) - 4 - 5
    chunks, rest = refs[:count], refs[count:]
    near_ref, query_ref, acc_ref, top_ref, *scratch = rest
    own = [ref[...] for ref in chunks[:queries]]
    near_ref[...] = query_rows(adj_ref, own, w_ref.shape[0])
    work = Work(gain_ref[...], w_ref, near_ref[...], query_ref, acc_ref, top_ref, scratch)
    work.project_queries(own)
    first = True
    for pieces in blocks_of(chunks[queries:], scratch[0].shape[0]):
        work.absorb(pieces, first)
        first = False


def next_kernel(near_ref, query_ref, acc_in, top_in, gain_ref, w_ref, *refs):
    count = len(refs) - 2 - 5
    chunks, rest = refs[:count], refs[count:]
    acc_ref, top_ref, *scratch = rest
    acc_ref[...] = acc_in[...]
    top_ref[...] = top_in[...]
    work = Work(gain_ref[...], w_ref, near_ref[...], query_ref, acc_ref, top_ref, scratch)
    for pieces in blocks_of(chunks, scratch[0].shape[0]):
        work.absorb(pieces, False)


def last_kernel(near_ref, query_ref, acc_in, top_in, gain_ref, w_ref, wo_ref, *refs):
    count = len(refs) - 4 - 5
    chunks, rest = refs[:count], refs[count:]
    out_ref, acc_ref, top_ref, att_ref, *scratch = rest
    acc_ref[...] = acc_in[...]
    top_ref[...] = top_in[...]
    work = Work(gain_ref[...], w_ref, near_ref[...], query_ref, acc_ref, top_ref, scratch)
    for pieces in blocks_of(chunks, scratch[0].shape[0]):
        work.absorb(pieces, False)
    for head in range(acc_ref.shape[0]):
        total = acc_ref[head, HEAD_DIM : HEAD_DIM + 1, :]
        part = acc_ref[head, :HEAD_DIM, :] / total
        att_ref[head * HEAD_DIM : (head + 1) * HEAD_DIM, :] = part.astype(jnp.bfloat16)
    attended = att_ref[...].T
    for start in range(0, attended.shape[1], COLS):
        out = dot(attended, wo_ref[:, start : start + COLS])
        out_ref[:, start : start + COLS] = out.astype(jnp.bfloat16)


def vmem(count):
    return [pl.BlockSpec(memory_space=pltpu.VMEM)] * count


def scratch(queries, heads):
    return [
        pltpu.VMEM((BLOCK, heads * HEAD_DIM), jnp.bfloat16),
        pltpu.VMEM((BLOCK, heads * HEAD_DIM), jnp.bfloat16),
        pltpu.VMEM((heads, VAL_ROWS, BLOCK), jnp.bfloat16),
        pltpu.VMEM((BLOCK, queries), jnp.float32),
        pltpu.VMEM((heads, BLOCK, queries), jnp.bfloat16),
    ]


def cost(queries, keys, width, more):
    flops = 2 * (2 * keys * width * width + 4 * queries * keys * width + more * queries * width * width)
    return pl.CostEstimate(flops=flops, bytes_accessed=8 * width * width, transcendentals=0)


PARAMS = pltpu.CompilerParams(vmem_limit_bytes=16 * 1024 * 1024)


def state_shapes(heads, queries):
    return (
        jax.ShapeDtypeStruct((heads, ACC_ROWS, queries), jnp.float32),
        jax.ShapeDtypeStruct((heads, queries), jnp.float32),
    )


def fetch_kernel(from_ref, after_ref, to_ref, sem):
    del after_ref
    copy = pltpu.make_async_copy(from_ref, to_ref, sem)
    copy.start()
    copy.wait()


def fetch(weights, after):
    return pl.pallas_call(
        fetch_kernel,
        out_shape=pltpu.VMEM(weights.shape, weights.dtype),
        in_specs=[pl.BlockSpec(memory_space=pltpu.HBM), pl.BlockSpec(memory_space=pl.ANY)],
        out_specs=pl.BlockSpec(memory_space=pl.ANY),
        scratch_shapes=[pltpu.SemaphoreType.DMA],
        compiler_params=pltpu.CompilerParams(vmem_limit_bytes=1024 * 1024),
        cost_estimate=pl.CostEstimate(flops=0, bytes_accessed=2 * weights.size * 2, transcendentals=0),
        name="fetch",
    )(weights, after)


def call_first(gain, adjacency, w_qkv, own, chunks):
    width, tiles = w_qkv.shape[0], adjacency.shape[0]
    queries = sum(chunk.shape[0] for chunk in own)
    heads = width // HEAD_DIM
    operands = (gain, adjacency, w_qkv, *own, *chunks)
    return pl.pallas_call(
        functools.partial(first_kernel, len(own)),
        out_shape=(
            jax.ShapeDtypeStruct((tiles, queries), jnp.bfloat16),
            jax.ShapeDtypeStruct((queries, width), jnp.bfloat16),
            *state_shapes(heads, queries),
        ),
        in_specs=vmem(len(operands)),
        out_specs=tuple(vmem(4)),
        scratch_shapes=scratch(queries, heads),
        compiler_params=PARAMS,
        cost_estimate=cost(queries, sum(c.shape[0] for c in chunks), width, 1),
        name="attend_first",
    )(*operands)


def call_next(near, query, acc, top, gain, w_qkv, chunks):
    queries, width = query.shape
    heads = width // HEAD_DIM
    operands = (near, query, acc, top, gain, w_qkv, *chunks)
    return pl.pallas_call(
        next_kernel,
        out_shape=state_shapes(heads, queries),
        in_specs=vmem(len(operands)),
        out_specs=tuple(vmem(2)),
        scratch_shapes=scratch(queries, heads),
        compiler_params=PARAMS,
        cost_estimate=cost(queries, sum(c.shape[0] for c in chunks), width, 0),
        name="attend_next",
    )(*operands)


def call_last(near, query, acc, top, gain, w_qkv, wo, chunks):
    queries, width = query.shape
    heads = width // HEAD_DIM
    operands = (near, query, acc, top, gain, w_qkv, wo, *chunks)
    return pl.pallas_call(
        last_kernel,
        out_shape=jax.ShapeDtypeStruct((queries, width), jnp.bfloat16),
        in_specs=vmem(len(operands)),
        out_specs=vmem(1)[0],
        scratch_shapes=[
            pltpu.VMEM((heads, ACC_ROWS, queries), jnp.float32),
            pltpu.VMEM((heads, queries), jnp.float32),
            pltpu.VMEM((width, queries), jnp.bfloat16),
            *scratch(queries, heads),
        ],
        compiler_params=PARAMS,
        cost_estimate=cost(queries, sum(c.shape[0] for c in chunks), width, 1),
        name="attend_last",
    )(*operands)


def on_device(cells_in, gain, w_qkv, w_out, tile_of_cell, tile_adjacent):
    genes, cell_dev, width = cells_in.shape
    head_devs, cell_devs = lax.axis_size("heads"), lax.axis_size("cells")
    sets = cell_devs // genes
    half = genes // 2
    gene = lax.rem(lax.axis_index("cells"), genes)
    same = [[s * genes + g for s in range(sets)] for g in range(genes)]

    def over_cells(value, step):
        return lax.ppermute(value, "cells", [(i, i ^ step) for i in range(cell_devs)])

    def over_heads(value, step):
        return lax.ppermute(value, "heads", [(i, i ^ step) for i in range(head_devs)])

    tags = jnp.broadcast_to(tile_of_cell.astype(jnp.bfloat16)[:, None], (cell_dev, TAG))

    def piece_for(k):
        rows = lax.dynamic_index_in_dim(cells_in, gene ^ k, 0, keepdims=False)
        return jnp.concatenate([rows, tags], axis=1)

    arrived = [piece_for(0)] + [None] * (genes - 1)
    for k in [*range(half, genes), *range(1, half)]:
        arrived[k] = over_cells(piece_for(k), k)
    own = [jnp.concatenate(arrived[:half], 0)]
    w_qkv, *late = lax.optimization_barrier((fetch(w_qkv, own[0]), *arrived[half:]))
    own.append(jnp.concatenate(late, 0))
    others, near_chunks = [[], []], []
    for i in range(2):
        held = own[i]
        if sets > 1:
            held = lax.all_gather(held, "cells", axis=0, axis_index_groups=same, tiled=True)
        near_chunks += [held, over_heads(held, 1)]
        for step in range(2, head_devs, 2):
            chunk = over_heads(held, step)
            others[i] += [chunk, over_heads(chunk, 1)] if i == 0 else [chunk, None]
    gain = gain.reshape(1, width)
    near, query, acc, top = call_first(gain, tile_adjacent, w_qkv, own, near_chunks)
    for step in range(2, head_devs, 2):
        chunk, acc = lax.optimization_barrier((others[1][step - 2], acc))
        others[1][step - 2 : step] = [chunk, over_heads(chunk, 1)]
    acc, top = call_next(near, query, acc, top, gain, w_qkv, others[0])
    out = call_last(near, query, acc, top, gain, w_qkv, w_out, others[1])
    out = out.reshape(genes, cell_dev, width)
    result = jnp.zeros_like(out)
    for k in [0, *range(half, genes), *range(1, half)]:
        piece = out[k] if k == 0 else over_cells(out[k], k)
        result = lax.dynamic_update_index_in_dim(result, piece, gene ^ k, 0)
    return result


def solution(mesh):
    return jax.shard_map(
        on_device,
        mesh=mesh,
        in_specs=(P(None, ("heads", "cells"), None), P(), P(), P(), P(("heads", "cells")), P()),
        out_specs=P(None, ("heads", "cells"), None),
        check_vma=False,
    )
```

```python
import math

import jax
import jax.numpy as jnp
from jax import lax
from jax.experimental import pallas as pl
from jax.experimental.pallas import tpu as pltpu
from jax.sharding import PartitionSpec as P

HEAD_DIM = 64
PAIR = 2 * HEAD_DIM
VAL_ROWS = PAIR + 16
ACC_ROWS = HEAD_DIM + 8
MASKED = -1e30
SCALE = 0.125 * math.log2(math.e)
COLS = 256
TAG = 128
BF16 = jnp.bfloat16
F32 = jnp.float32


def dot(a, b, a_dim=1, b_dim=0):
    return lax.dot_general(a, b, (((a_dim,), (b_dim,)), ((), ())), preferred_element_type=F32)


def one_hot(tags, count):
    tags = tags.astype(F32)
    lane = lax.broadcasted_iota(jnp.int32, tags.shape, 1).astype(F32)
    parts = [(tags == lane + start).astype(F32) for start in range(0, count, TAG)]
    return jnp.concatenate(parts, axis=1).astype(BF16)


class Stage:
    def __init__(self, env, pieces, queries, blocks, attend, fetch=False, finish=False, keep=()):
        self.pieces, self.queries, self.blocks = pieces, queries, blocks
        self.attend, self.fetch, self.finish, self.keep = attend, fetch, finish, keep
        self.width = env["w_hbm"].shape[0]
        self.tiles = env["adjacency_hbm"].shape[0]
        self.pairs = self.width // PAIR
        self.rows = {q: sum(size for _, _, size in pieces["q", q]) for q in {q for q, _ in attend}}
        self.cells = {b: sum(size for _, _, size in pieces["k", b]) for b in {b for _, b in attend}}
        self.block = max(self.cells.values())
        self.touched = sorted({q for q, _ in attend})
        ins = {"w_hbm", "gain_hbm", "adjacency_hbm"} if fetch else {"w"}
        if queries and not fetch:
            ins.add("adjacency")
        for group in [("q", q) for q in queries] + [("k", b) for b in {b for _, b in attend}]:
            ins |= {name for name, _, _ in pieces[group]}
        for q in self.touched:
            if q not in queries:
                ins |= {f"Q{q}", f"G{q}"}
            if f"acc{q}" in env:
                ins |= {f"acc{q}", f"top{q}"}
        for b in {b for _, b in attend} - set(blocks):
            ins |= {f"K{b}", f"V{b}"}
        if finish:
            ins.add("w_out")
        self.ins = sorted(ins)
        self.held = set(ins)
        shapes = {}
        for q in queries:
            shapes[f"Q{q}"] = ((self.pairs, 2 * self.rows[q], PAIR), BF16)
            shapes[f"G{q}"] = ((self.tiles, 2 * self.rows[q]), BF16)
        for q in self.touched:
            shapes[f"acc{q}"] = ((self.pairs, ACC_ROWS, 2 * self.rows[q]), F32)
            shapes[f"top{q}"] = ((self.pairs, 2 * self.rows[q]), F32)
        for b in blocks:
            shapes[f"K{b}"] = ((self.cells[b], self.width), BF16)
            shapes[f"V{b}"] = ((self.pairs, VAL_ROWS, self.cells[b]), BF16)
        outs, scratch = {}, {}
        for name, shape in shapes.items():
            stays = name[0] in "KV" and int(name[1:]) not in keep
            (scratch if finish or stays else outs)[name] = shape
        if finish:
            for q in self.touched:
                outs[f"out{q}"] = ((self.rows[q], self.width), BF16)
        self.outs, self.scratch = outs, scratch

    def body(self, *refs):
        count = len(self.ins)
        names = list(self.outs) + ["adjacency", "w"] * self.fetch + list(self.scratch)
        more = ["cells", "bias", "weights"] + ["attended"] * self.finish
        more += ["gain", "pairs_allowed", "sems"] * self.fetch
        self.read = dict(zip(self.ins, refs[:count]))
        self.write = dict(zip(names + more, refs[count:]))
        self.w = self.write["w"] if self.fetch else self.read["w"]
        if self.fetch:
            self.start_copies()
        for b in self.blocks:
            root = self.load_cells("k", b)
            if self.fetch and b == self.blocks[0]:
                self.take_weights(1)
            self.project_keys(b, root)
            if self.fetch and b == self.blocks[0]:
                self.take_weights(2)
            self.project_values(b, root)
        if self.fetch:
            self.take_weights(0)
        for q in self.queries:
            self.project_queries(q)
        self.attend_all()
        if self.finish:
            for q in self.touched:
                self.project_out(q)

    def ref(self, name):
        return self.write[name] if name in self.write else self.read[name]

    def rows_of(self, kind, index, columns):
        parts = self.pieces[kind, index]
        return [self.read[name][start : start + size, columns] for name, start, size in parts]

    def start_copies(self):
        width, sems = self.width, self.write["sems"]
        moves = [(self.read["gain_hbm"], self.write["gain"])]
        moves += [(self.read["adjacency_hbm"], self.write["pairs_allowed"])]
        for start in (width, 2 * width, 0):
            part = slice(start, start + width)
            moves.append((self.read["w_hbm"].at[:, part], self.write["w"].at[:, part]))
        copies = [pltpu.make_async_copy(*move, sems.at[i]) for i, move in enumerate(moves)]
        for copy in copies:
            copy.start()
        copies[0].wait()
        self.copies = {1: copies[2], 2: copies[3], 0: copies[4]}
        self.gain = self.write["gain"][...].T
        copies[1].wait()
        allowed = self.write["pairs_allowed"][...]
        self.write["adjacency"][...] = allowed.astype(F32).astype(BF16)

    def take_weights(self, part):
        self.copies[part].wait()
        columns = slice(part * self.width, (part + 1) * self.width)
        size = self.gain.shape[0]
        for i in range(self.width // size):
            rows = slice(i * size, (i + 1) * size)
            scaled = self.w[rows, columns].astype(F32) * self.gain[:, i : i + 1]
            self.w[rows, columns] = scaled.astype(BF16)

    def load_cells(self, kind, index):
        start, roots = 0, []
        for rows in self.rows_of(kind, index, slice(0, self.width)):
            self.write["cells"][start : start + rows.shape[0], :] = rows
            start += rows.shape[0]
            x32 = rows.astype(F32)
            roots.append(lax.rsqrt(jnp.mean(x32 * x32, axis=-1, keepdims=True) + 1e-05))
        return jnp.concatenate(roots, axis=0)

    def tags_of(self, kind, index):
        tags = jnp.concatenate(self.rows_of(kind, index, slice(self.width, None)), axis=0)
        return one_hot(tags, self.tiles)

    def project_queries(self, q):
        rows = self.rows[q]
        scale = self.load_cells("q", q) * SCALE
        cells = self.write["cells"][:rows, :]
        for start in range(0, self.width, COLS):
            query = (dot(cells, self.w[:, start : start + COLS]) * scale).astype(BF16)
            lane = lax.broadcasted_iota(jnp.int32, (rows, PAIR), 1)
            for part in range(COLS // PAIR):
                both = query[:, part * PAIR : (part + 1) * PAIR]
                pair = start // PAIR + part
                none = jnp.zeros_like(both)
                self.write[f"Q{q}"][pair, :rows, :] = jnp.where(lane < HEAD_DIM, both, none)
                self.write[f"Q{q}"][pair, rows:, :] = jnp.where(lane < HEAD_DIM, none, both)
        near = dot(self.ref("adjacency")[...], self.tags_of("q", q), 1, 1).astype(BF16)
        self.write[f"G{q}"][...] = jnp.concatenate([near, near], axis=1)

    def project_keys(self, b, root):
        cells = self.write["cells"][: self.cells[b], :]
        for start in range(0, self.width, COLS):
            part = slice(self.width + start, self.width + start + COLS)
            self.write[f"K{b}"][:, start : start + COLS] = (dot(cells, self.w[:, part]) * root).astype(BF16)

    def project_values(self, b, root):
        cells = self.write["cells"][: self.cells[b], :]
        ones = jnp.ones((self.pairs, VAL_ROWS - PAIR, self.cells[b]), BF16)
        self.write[f"V{b}"][:, PAIR:, :] = ones
        for start in range(0, self.width, COLS):
            part = slice(2 * self.width + start, 2 * self.width + start + COLS)
            values = (dot(cells, self.w[:, part]) * root).astype(BF16).T
            for i in range(COLS // PAIR):
                rows = values[i * PAIR : (i + 1) * PAIR]
                self.write[f"V{b}"][start // PAIR + i, :PAIR, :] = rows

    def attend_all(self):
        source = {q: self.read for q in self.touched if f"acc{q}" in self.held}
        before = None
        for turn, (q, b) in enumerate(self.attend):
            after = self.start_turn(q, b, source.get(q), turn % 2)
            source[q] = self.write
            for pair in range(self.pairs):
                self.weigh(after, pair)
                if before is not None:
                    self.add_values(before, pair)
            before = after
        for pair in range(self.pairs):
            self.add_values(before, pair)

    def start_turn(self, q, b, before, slot):
        cells = self.cells[b]
        bias_ref = self.write["bias"].at[slot, :cells]
        bias_ref[...] = (dot(self.tags_of("k", b), self.ref(f"G{q}")[...]) - 1.0) * -MASKED
        return (q, b, before, bias_ref, self.write["weights"].at[slot, :, :cells], {})

    def weigh(self, turn, pair):
        q, b, before, bias_ref, weight_ref, factors = turn
        keys = self.ref(f"K{b}")[:, pair * PAIR : (pair + 1) * PAIR]
        scores = dot(keys, self.ref(f"Q{q}")[pair], 1, 1) + bias_ref[...]
        top = jnp.max(scores, axis=0, keepdims=True)
        if before is not None:
            last = before[f"top{q}"][pair : pair + 1, :]
            top = jnp.maximum(top, last)
            factors[pair] = jnp.exp2(last - top)
        weight_ref[pair] = jnp.exp2(scores - top).astype(BF16)
        self.write[f"top{q}"][pair : pair + 1, :] = top

    def add_values(self, turn, pair):
        q, b, before, _, weight_ref, factors = turn
        half = self.rows[q]
        acc_ref = self.write[f"acc{q}"]
        summed = dot(self.ref(f"V{b}")[pair], weight_ref[pair])
        even, odd = summed[:HEAD_DIM, :half], summed[HEAD_DIM:PAIR, half:]
        both = jnp.concatenate([even, odd], axis=1)
        total = summed[PAIR : PAIR + ACC_ROWS - HEAD_DIM]
        if before is not None:
            both = both + before[f"acc{q}"][pair, :HEAD_DIM, :] * factors[pair]
            total = total + before[f"acc{q}"][pair, HEAD_DIM:, :] * factors[pair]
        acc_ref[pair, :HEAD_DIM, :] = both
        acc_ref[pair, HEAD_DIM:, :] = total

    def project_out(self, q):
        half = self.rows[q]
        acc_ref, att_ref = self.write[f"acc{q}"], self.write["attended"]
        for pair in range(self.pairs):
            total = acc_ref[pair, HEAD_DIM : HEAD_DIM + 1, :]
            part = (acc_ref[pair, :HEAD_DIM, :] / total).astype(BF16)
            row = pair * PAIR
            att_ref[row : row + HEAD_DIM, :] = part[:, :half]
            att_ref[row + HEAD_DIM : row + PAIR, :] = part[:, half:]
        attended = att_ref[...].T
        for start in range(0, self.width, COLS):
            out = dot(attended, self.read["w_out"][:, start : start + COLS]).astype(BF16)
            self.write[f"out{q}"][:, start : start + COLS] = out

    def call(self, env, name):
        vmem = pl.BlockSpec(memory_space=pltpu.VMEM)
        hbm = pl.BlockSpec(memory_space=pltpu.HBM)
        operands = [env[n] for n in self.ins]
        out_shape = [jax.ShapeDtypeStruct(*shape) for shape in self.outs.values()]
        out_specs = [vmem] * len(out_shape)
        rows = max(self.rows.values())
        scratch = [pltpu.VMEM(*shape) for shape in self.scratch.values()]
        scratch += [
            pltpu.VMEM((max(self.block, rows), self.width), BF16),
            pltpu.VMEM((2, self.block, 2 * rows), F32),
            pltpu.VMEM((2, self.pairs, self.block, 2 * rows), BF16),
        ]
        if self.finish:
            scratch.append(pltpu.VMEM((self.width, rows), BF16))
        if self.fetch:
            shape = (self.width, 3 * self.width)
            out_shape += [jax.ShapeDtypeStruct((self.tiles, self.tiles), BF16), pltpu.VMEM(shape, BF16)]
            out_specs += [vmem, vmem]
            scratch += [
                pltpu.VMEM(env["gain_hbm"].shape, F32),
                pltpu.VMEM((self.tiles, self.tiles), jnp.int32),
                pltpu.SemaphoreType.DMA((5,)),
            ]
        flops = 2 * self.width * (
            2 * sum(self.cells[b] for b in self.blocks) * self.width
            + (len(self.queries) + self.finish * len(self.touched)) * rows * self.width
            + 8 * sum(self.cells[b] for _, b in self.attend) * rows
        )
        outs = pl.pallas_call(
            self.body,
            out_shape=tuple(out_shape),
            in_specs=[hbm if n.endswith("_hbm") else vmem for n in self.ins],
            out_specs=tuple(out_specs),
            scratch_shapes=scratch,
            compiler_params=pltpu.CompilerParams(vmem_limit_bytes=16 * 1024 * 1024),
            cost_estimate=pl.CostEstimate(flops=flops, bytes_accessed=1 << 23, transcendentals=0),
            name=name,
        )(*operands)
        env.update(zip(list(self.outs) + ["adjacency", "w"] * self.fetch, outs))


def on_device(cells_in, gain, w_qkv, w_out, tile_of_cell, tile_adjacent):
    genes, cell_dev, width = cells_in.shape
    head_devs, cell_devs = lax.axis_size("heads"), lax.axis_size("cells")
    sets = cell_devs // genes
    half = genes // 2
    gene = lax.rem(lax.axis_index("cells"), genes)
    same = [[s * genes + g for s in range(sets)] for g in range(genes)]

    def over_cells(value, step):
        return lax.ppermute(value, "cells", [(i, i ^ step) for i in range(cell_devs)])

    def over_heads(value, step):
        return lax.ppermute(value, "heads", [(i, i ^ step) for i in range(head_devs)])

    tags = jnp.broadcast_to(tile_of_cell.astype(BF16)[:, None], (cell_dev, TAG))

    def piece_for(k):
        rows = lax.dynamic_index_in_dim(cells_in, gene ^ k, 0, keepdims=False)
        return jnp.concatenate([rows, tags], axis=1)

    order = [4, 1, 2, 0, 6, 5, 7, 3] if genes == 8 else list(range(genes))
    arrived = [over_cells(piece_for(k), k) if k else piece_for(0) for k in order]
    env = {"w_out": w_out}
    held = {"w_hbm": w_qkv, "gain_hbm": gain.reshape(-1, TAG), "adjacency_hbm": tile_adjacent}
    for name, value in held.items():
        env[name] = pltpu.with_memory_space_constraint(value, pltpu.HBM)
    pieces = {}
    rows = half * cell_dev

    def spread(group, own, beside):
        env[f"own{group}"] = own
        pieces["q", group] = [(f"own{group}", 0, rows)]
        held = own
        if sets > 1:
            held = lax.all_gather(own, "cells", axis=0, axis_index_groups=same, tiled=True)
        for step in range(0, head_devs, 2):
            env[f"chunk{group}{step}"] = over_heads(held, step) if step else held
            if step in beside:
                env[f"beside{group}{step}"] = over_heads(env[f"chunk{group}{step}"], 1)

    first = jnp.concatenate(arrived[:half], 0)
    steps = range(0, head_devs, 2)
    spread(0, first, steps)
    if sets == 1 and head_devs == 4:
        blocks = [["own0"], ["beside00", "own1"], ["beside10", "chunk02"], ["beside02", "chunk12"], ["beside12"]]
        for b, names in enumerate(blocks):
            pieces["k", b] = [(name, 0, rows) for name in names]
        Stage(env, pieces, [0], [0], [(0, 0)], fetch=True, keep=[0]).call(env, "first_group")
        env["w"], *late = lax.optimization_barrier((env["w"], *arrived[half:]))
        spread(1, jnp.concatenate(late, 0), [0])
        attend = [(0, 1), (1, 0), (1, 1), (0, 2), (1, 2)]
        Stage(env, pieces, [1], [1, 2], attend).call(env, "second_group")
        env["chunk12"], env["top1"] = lax.optimization_barrier((env["chunk12"], env["top1"]))
        env["beside12"] = over_heads(env["chunk12"], 1)
        Stage(env, pieces, [], [3], [(0, 3), (1, 3)]).call(env, "far")
        Stage(env, pieces, [], [4], [(0, 4), (1, 4)], finish=True).call(env, "last")
    else:
        spread(1, jnp.concatenate(arrived[half:], 0), steps)
        names = [f"{kind}{group}{step}" for group in range(2) for step in steps for kind in ("chunk", "beside")]
        for b, (name, s) in enumerate((name, s) for name in names for s in range(sets)):
            pieces["k", b] = [(name, s * rows, rows)]
        last = len(names) * sets - 1
        for b in range(last + 1):
            attend = [(0, b), (1, b)]
            stage = Stage(env, pieces, [] if b else [0, 1], [b], attend, fetch=b == 0, finish=b == last)
            stage.call(env, f"block_{b}")
    result = jnp.zeros_like(cells_in)
    for place, k in enumerate(order):
        start = place % half * cell_dev
        piece = env[f"out{place // half}"][start : start + cell_dev]
        piece = over_cells(piece, k) if k else piece
        result = lax.dynamic_update_index_in_dim(result, piece, gene ^ k, 0)
    return result


def solution(mesh):
    return jax.shard_map(
        on_device,
        mesh=mesh,
        in_specs=(P(None, ("heads", "cells"), None), P(), P(), P(), P(("heads", "cells")), P()),
        out_specs=P(None, ("heads", "cells"), None),
        check_vma=False,
    )
```

```python
import math

import jax
import jax.numpy as jnp
from jax import lax
from jax.experimental import pallas as pl
from jax.experimental.pallas import tpu as pltpu
from jax.sharding import PartitionSpec as P

HEAD_DIM = 64
PAIR = 2 * HEAD_DIM
VAL_ROWS = PAIR + 16
ACC_ROWS = HEAD_DIM + 8
MASKED = -1e30
SCALE = 0.125 * math.log2(math.e)
COLS = 256
TAG = 128
BF16 = jnp.bfloat16
F32 = jnp.float32


def dot(a, b, a_dim=1, b_dim=0):
    return lax.dot_general(a, b, (((a_dim,), (b_dim,)), ((), ())), preferred_element_type=F32)


def one_hot(tags, count):
    tags = tags.astype(F32)
    lane = lax.broadcasted_iota(jnp.int32, tags.shape, 1).astype(F32)
    parts = [(tags == lane + start).astype(F32) for start in range(0, count, TAG)]
    return jnp.concatenate(parts, axis=1).astype(BF16)


def pack_kernel(order, x_hbm, gain_hbm, tile_hbm, *refs):
    out_refs, (cells_ref, gain_ref, tile_ref, sems) = refs[: len(order)], refs[len(order) :]
    genes, rows, width = cells_ref.shape
    gene = lax.rem(lax.axis_index("cells"), genes)
    moves = [(gain_hbm, gain_ref), (tile_hbm, tile_ref)]
    moves += [(x_hbm.at[gene ^ k], cells_ref.at[i]) for i, k in enumerate(order)]
    copies = [pltpu.make_async_copy(*move, sems.at[i]) for i, move in enumerate(moves)]
    for copy in copies:
        copy.start()
    for copy in copies:
        copy.wait()
    gain = gain_ref[...]
    row = lax.broadcasted_iota(jnp.int32, (rows, rows), 0)
    column = lax.broadcasted_iota(jnp.int32, (rows, rows), 1)
    tiles = jnp.where(row == column, tile_ref[...].astype(F32), 0.0)
    tags = jnp.broadcast_to(jnp.sum(tiles, axis=1, keepdims=True), (rows, TAG)).astype(BF16)
    for i in range(genes):
        x32 = cells_ref[i].astype(F32)
        mean = jnp.mean(x32 * x32, axis=-1, keepdims=True)
        out_refs[i][:, :width] = (x32 * lax.rsqrt(mean + 1e-05) * gain).astype(BF16)
        out_refs[i][:, width:] = tags


def pack(cells_in, gain, tiles, order):
    genes, rows, width = cells_in.shape
    operands = [cells_in, gain.reshape(1, width), tiles.reshape(1, rows)]
    operands = [pltpu.with_memory_space_constraint(value, pltpu.HBM) for value in operands]
    return pl.pallas_call(
        lambda *refs: pack_kernel(order, *refs),
        out_shape=[jax.ShapeDtypeStruct((rows, width + TAG), BF16)] * genes,
        in_specs=[pl.BlockSpec(memory_space=pltpu.HBM)] * 3,
        out_specs=[pl.BlockSpec(memory_space=pltpu.VMEM)] * genes,
        scratch_shapes=[
            pltpu.VMEM(cells_in.shape, BF16),
            pltpu.VMEM((1, width), F32),
            pltpu.VMEM((1, rows), jnp.int32),
            pltpu.SemaphoreType.DMA((genes + 2,)),
        ],
        compiler_params=pltpu.CompilerParams(vmem_limit_bytes=4 * 1024 * 1024),
        name="pack",
    )(*operands)


def unpack_kernel(order, *refs):
    piece_refs, (out_hbm, sems) = refs[: len(order)], refs[len(order) :]
    gene = lax.rem(lax.axis_index("cells"), len(order))
    copies = []
    for i, (k, piece_ref) in enumerate(zip(order, piece_refs)):
        copies.append(pltpu.make_async_copy(piece_ref, out_hbm.at[gene ^ k], sems.at[i]))
        copies[-1].start()
    for copy in copies:
        copy.wait()


def unpack(pieces, order, shape):
    return pl.pallas_call(
        lambda *refs: unpack_kernel(order, *refs),
        out_shape=jax.ShapeDtypeStruct(shape, BF16),
        in_specs=[pl.BlockSpec(memory_space=pl.ANY)] * len(order),
        out_specs=pl.BlockSpec(memory_space=pltpu.HBM),
        scratch_shapes=[pltpu.SemaphoreType.DMA((len(order),))],
        compiler_params=pltpu.CompilerParams(vmem_limit_bytes=1024 * 1024),
        name="unpack",
    )(*pieces)


class Stage:
    def __init__(self, env, pieces, queries, blocks, attend, fetch=False, finish=False, keep=()):
        self.pieces, self.queries, self.blocks = pieces, queries, blocks
        self.attend, self.fetch, self.finish, self.keep = attend, fetch, finish, keep
        self.width = env["w_hbm"].shape[0]
        self.tiles = env["adjacency_hbm"].shape[0]
        self.pairs = self.width // PAIR
        self.rows = {q: sum(size for _, _, size in pieces["q", q]) for q in {q for q, _ in attend}}
        self.cells = {b: sum(size for _, _, size in pieces["k", b]) for b in {b for _, b in attend}}
        self.block = max(self.cells.values())
        self.touched = sorted({q for q, _ in attend})
        ins = {"w_hbm", "adjacency_hbm"} if fetch else {"w"}
        if queries and not fetch:
            ins.add("adjacency")
        for group in [("q", q) for q in queries] + [("k", b) for b in {b for _, b in attend}]:
            ins |= {name for name, _, _ in pieces[group]}
        for q in self.touched:
            if q not in queries:
                ins |= {f"Q{q}", f"G{q}"}
            if f"acc{q}" in env:
                ins |= {f"acc{q}", f"top{q}"}
        for b in {b for _, b in attend} - set(blocks):
            ins |= {f"K{b}", f"V{b}"}
        if finish:
            ins.add("w_out")
        self.ins = sorted(ins)
        self.held = set(ins)
        shapes = {}
        for q in queries:
            shapes[f"Q{q}"] = ((self.pairs, 2 * self.rows[q], PAIR), BF16)
            shapes[f"G{q}"] = ((self.tiles, 2 * self.rows[q]), BF16)
        for q in self.touched:
            shapes[f"acc{q}"] = ((self.pairs, ACC_ROWS, 2 * self.rows[q]), F32)
            shapes[f"top{q}"] = ((self.pairs, 2 * self.rows[q]), F32)
        for b in blocks:
            shapes[f"K{b}"] = ((self.cells[b], self.width), BF16)
            shapes[f"V{b}"] = ((self.pairs, VAL_ROWS, self.cells[b]), BF16)
        outs, scratch = {}, {}
        for name, shape in shapes.items():
            stays = name[0] in "KV" and int(name[1:]) not in keep
            (scratch if finish or stays else outs)[name] = shape
        if finish:
            for q in self.touched:
                outs[f"out{q}"] = ((self.rows[q], self.width), BF16)
        self.outs, self.scratch = outs, scratch

    def body(self, *refs):
        count = len(self.ins)
        names = list(self.outs) + ["adjacency", "w"] * self.fetch + list(self.scratch)
        more = ["bias", "weights"] + ["attended"] * self.finish
        more += ["pairs_allowed", "sems"] * self.fetch
        self.read = dict(zip(self.ins, refs[:count]))
        self.write = dict(zip(names + more, refs[count:]))
        self.w = self.write["w"] if self.fetch else self.read["w"]
        if self.fetch:
            self.start_copies()
        for b in self.blocks:
            cells = self.load_cells("k", b)
            if self.fetch and b == self.blocks[0]:
                self.copies[1].wait()
            self.project_keys(b, cells)
            if self.fetch and b == self.blocks[0]:
                self.copies[2].wait()
            self.project_values(b, cells)
        if self.fetch:
            self.copies[0].wait()
        for q in self.queries:
            self.project_queries(q)
        self.attend_all()
        if self.finish:
            for q in self.touched:
                self.project_out(q)

    def ref(self, name):
        return self.write[name] if name in self.write else self.read[name]

    def rows_of(self, kind, index, columns):
        parts = self.pieces[kind, index]
        return [self.read[name][start : start + size, columns] for name, start, size in parts]

    def start_copies(self):
        width, sems = self.width, self.write["sems"]
        moves = [(self.read["adjacency_hbm"], self.write["pairs_allowed"])]
        for start in (width, 2 * width, 0):
            part = slice(start, start + width)
            moves.append((self.read["w_hbm"].at[:, part], self.write["w"].at[:, part]))
        copies = [pltpu.make_async_copy(*move, sems.at[i]) for i, move in enumerate(moves)]
        for copy in copies:
            copy.start()
        copies[0].wait()
        self.copies = {1: copies[1], 2: copies[2], 0: copies[3]}
        allowed = self.write["pairs_allowed"][...]
        self.write["adjacency"][...] = allowed.astype(F32).astype(BF16)

    def load_cells(self, kind, index):
        return jnp.concatenate(self.rows_of(kind, index, slice(0, self.width)), axis=0)

    def tags_of(self, kind, index):
        tags = jnp.concatenate(self.rows_of(kind, index, slice(self.width, None)), axis=0)
        return one_hot(tags, self.tiles)

    def project_queries(self, q):
        rows = self.rows[q]
        cells = self.load_cells("q", q)
        for start in range(0, self.width, COLS):
            query = (dot(cells, self.w[:, start : start + COLS]) * SCALE).astype(BF16)
            lane = lax.broadcasted_iota(jnp.int32, (rows, PAIR), 1)
            for part in range(COLS // PAIR):
                both = query[:, part * PAIR : (part + 1) * PAIR]
                pair = start // PAIR + part
                none = jnp.zeros_like(both)
                self.write[f"Q{q}"][pair, :rows, :] = jnp.where(lane < HEAD_DIM, both, none)
                self.write[f"Q{q}"][pair, rows:, :] = jnp.where(lane < HEAD_DIM, none, both)
        near = dot(self.ref("adjacency")[...], self.tags_of("q", q), 1, 1).astype(BF16)
        self.write[f"G{q}"][...] = jnp.concatenate([near, near], axis=1)

    def project_keys(self, b, cells):
        for start in range(0, self.width, COLS):
            part = slice(self.width + start, self.width + start + COLS)
            self.write[f"K{b}"][:, start : start + COLS] = dot(cells, self.w[:, part]).astype(BF16)

    def project_values(self, b, cells):
        ones = jnp.ones((self.pairs, VAL_ROWS - PAIR, self.cells[b]), BF16)
        self.write[f"V{b}"][:, PAIR:, :] = ones
        for start in range(0, self.width, COLS):
            part = slice(2 * self.width + start, 2 * self.width + start + COLS)
            values = dot(cells, self.w[:, part]).astype(BF16).T
            for i in range(COLS // PAIR):
                rows = values[i * PAIR : (i + 1) * PAIR]
                self.write[f"V{b}"][start // PAIR + i, :PAIR, :] = rows

    def attend_all(self):
        source = {q: self.read for q in self.touched if f"acc{q}" in self.held}
        before = None
        for turn, (q, b) in enumerate(self.attend):
            after = self.start_turn(q, b, source.get(q), turn % 2)
            source[q] = self.write
            for pair in range(self.pairs):
                self.weigh(after, pair)
                if before is not None:
                    self.add_values(before, pair)
            before = after
        for pair in range(self.pairs):
            self.add_values(before, pair)

    def start_turn(self, q, b, before, slot):
        cells = self.cells[b]
        bias_ref = self.write["bias"].at[slot, :cells]
        bias_ref[...] = (dot(self.tags_of("k", b), self.ref(f"G{q}")[...]) - 1.0) * -MASKED
        return (q, b, before, bias_ref, self.write["weights"].at[slot, :, :cells], {})

    def weigh(self, turn, pair):
        q, b, before, bias_ref, weight_ref, factors = turn
        keys = self.ref(f"K{b}")[:, pair * PAIR : (pair + 1) * PAIR]
        scores = dot(keys, self.ref(f"Q{q}")[pair], 1, 1) + bias_ref[...]
        top = jnp.max(scores, axis=0, keepdims=True)
        if before is not None:
            last = before[f"top{q}"][pair : pair + 1, :]
            top = jnp.maximum(top, last)
            factors[pair] = jnp.exp2(last - top)
        weight_ref[pair] = jnp.exp2(scores - top).astype(BF16)
        self.write[f"top{q}"][pair : pair + 1, :] = top

    def add_values(self, turn, pair):
        q, b, before, _, weight_ref, factors = turn
        half = self.rows[q]
        acc_ref = self.write[f"acc{q}"]
        summed = dot(self.ref(f"V{b}")[pair], weight_ref[pair])
        even, odd = summed[:HEAD_DIM, :half], summed[HEAD_DIM:PAIR, half:]
        both = jnp.concatenate([even, odd], axis=1)
        total = summed[PAIR : PAIR + ACC_ROWS - HEAD_DIM]
        if before is not None:
            both = both + before[f"acc{q}"][pair, :HEAD_DIM, :] * factors[pair]
            total = total + before[f"acc{q}"][pair, HEAD_DIM:, :] * factors[pair]
        acc_ref[pair, :HEAD_DIM, :] = both
        acc_ref[pair, HEAD_DIM:, :] = total

    def project_out(self, q):
        half = self.rows[q]
        acc_ref, att_ref = self.write[f"acc{q}"], self.write["attended"]
        for pair in range(self.pairs):
            total = acc_ref[pair, HEAD_DIM : HEAD_DIM + 1, :]
            part = (acc_ref[pair, :HEAD_DIM, :] / total).astype(BF16)
            row = pair * PAIR
            att_ref[row : row + HEAD_DIM, :] = part[:, :half]
            att_ref[row + HEAD_DIM : row + PAIR, :] = part[:, half:]
        attended = att_ref[...].T
        for start in range(0, self.width, COLS):
            out = dot(attended, self.read["w_out"][:, start : start + COLS]).astype(BF16)
            self.write[f"out{q}"][:, start : start + COLS] = out

    def call(self, env, name):
        vmem = pl.BlockSpec(memory_space=pltpu.VMEM)
        hbm = pl.BlockSpec(memory_space=pltpu.HBM)
        operands = [env[n] for n in self.ins]
        out_shape = [jax.ShapeDtypeStruct(*shape) for shape in self.outs.values()]
        out_specs = [vmem] * len(out_shape)
        rows = max(self.rows.values())
        scratch = [pltpu.VMEM(*shape) for shape in self.scratch.values()]
        scratch += [
            pltpu.VMEM((2, self.block, 2 * rows), F32),
            pltpu.VMEM((2, self.pairs, self.block, 2 * rows), BF16),
        ]
        if self.finish:
            scratch.append(pltpu.VMEM((self.width, rows), BF16))
        if self.fetch:
            shape = (self.width, 3 * self.width)
            out_shape += [jax.ShapeDtypeStruct((self.tiles, self.tiles), BF16), pltpu.VMEM(shape, BF16)]
            out_specs += [vmem, vmem]
            scratch += [
                pltpu.VMEM((self.tiles, self.tiles), jnp.int32),
                pltpu.SemaphoreType.DMA((4,)),
            ]
        flops = 2 * self.width * (
            2 * sum(self.cells[b] for b in self.blocks) * self.width
            + (len(self.queries) + self.finish * len(self.touched)) * rows * self.width
            + 8 * sum(self.cells[b] for _, b in self.attend) * rows
        )
        outs = pl.pallas_call(
            self.body,
            out_shape=tuple(out_shape),
            in_specs=[hbm if n.endswith("_hbm") else vmem for n in self.ins],
            out_specs=tuple(out_specs),
            scratch_shapes=scratch,
            compiler_params=pltpu.CompilerParams(vmem_limit_bytes=16 * 1024 * 1024),
            cost_estimate=pl.CostEstimate(flops=flops, bytes_accessed=1 << 23, transcendentals=0),
            name=name,
        )(*operands)
        env.update(zip(list(self.outs) + ["adjacency", "w"] * self.fetch, outs))


def on_device(cells_in, gain, w_qkv, w_out, tile_of_cell, tile_adjacent):
    genes, cell_dev, width = cells_in.shape
    head_devs, cell_devs = lax.axis_size("heads"), lax.axis_size("cells")
    sets = cell_devs // genes
    half = genes // 2
    same = [[s * genes + g for s in range(sets)] for g in range(genes)]

    def over_cells(value, step):
        return lax.ppermute(value, "cells", [(i, i ^ step) for i in range(cell_devs)])

    def over_heads(value, step):
        return lax.ppermute(value, "heads", [(i, i ^ step) for i in range(head_devs)])

    order = [4, 1, 3, 0, 5, 7, 6, 2] if genes == 8 else list(range(genes))
    back = [0, 4, 1, 2, 6, 5, 7, 3] if genes == 8 else order
    packed = pack(cells_in, gain, tile_of_cell, order)
    arrived = [over_cells(piece, k) if k else piece for piece, k in zip(packed, order)]
    env = {"w_out": w_out}
    held = {"w_hbm": w_qkv, "adjacency_hbm": tile_adjacent}
    for name, value in held.items():
        env[name] = pltpu.with_memory_space_constraint(value, pltpu.HBM)
    pieces = {}
    rows = half * cell_dev

    def spread(group, own, beside):
        env[f"own{group}"] = own
        pieces["q", group] = [(f"own{group}", 0, rows)]
        held = own
        if sets > 1:
            held = lax.all_gather(own, "cells", axis=0, axis_index_groups=same, tiled=True)
        for step in range(0, head_devs, 2):
            env[f"chunk{group}{step}"] = over_heads(held, step) if step else held
            if step in beside:
                env[f"beside{group}{step}"] = over_heads(env[f"chunk{group}{step}"], 1)

    first = jnp.concatenate(arrived[:half], 0)
    steps = range(0, head_devs, 2)
    spread(0, first, steps)
    if sets == 1 and head_devs == 4:
        blocks = [["own0"], ["beside00", "own1"], ["beside10", "chunk02"], ["beside02", "chunk12"], ["beside12"]]
        for b, names in enumerate(blocks):
            pieces["k", b] = [(name, 0, rows) for name in names]
        Stage(env, pieces, [0], [0], [(0, 0)], fetch=True, keep=[0]).call(env, "first_group")
        env["w"], *late = lax.optimization_barrier((env["w"], *arrived[half:]))
        spread(1, jnp.concatenate(late, 0), [0])
        attend = [(0, 1), (1, 0), (1, 1), (0, 2), (1, 2)]
        Stage(env, pieces, [1], [1, 2], attend).call(env, "second_group")
        env["chunk12"], env["top1"] = lax.optimization_barrier((env["chunk12"], env["top1"]))
        env["beside12"] = over_heads(env["chunk12"], 1)
        Stage(env, pieces, [], [3], [(0, 3), (1, 3)]).call(env, "far")
        Stage(env, pieces, [], [4], [(0, 4), (1, 4)], finish=True).call(env, "last")
    else:
        spread(1, jnp.concatenate(arrived[half:], 0), steps)
        names = [f"{kind}{group}{step}" for group in range(2) for step in steps for kind in ("chunk", "beside")]
        for b, (name, s) in enumerate((name, s) for name in names for s in range(sets)):
            pieces["k", b] = [(name, s * rows, rows)]
        last = len(names) * sets - 1
        for b in range(last + 1):
            attend = [(0, b), (1, b)]
            stage = Stage(env, pieces, [] if b else [0, 1], [b], attend, fetch=b == 0, finish=b == last)
            stage.call(env, f"block_{b}")
    returned = []
    for k in back:
        place = order.index(k)
        start = place % half * cell_dev
        piece = env[f"out{place // half}"][start : start + cell_dev]
        returned.append(over_cells(piece, k) if k else piece)
    return unpack(returned, back, cells_in.shape)


def solution(mesh):
    return jax.shard_map(
        on_device,
        mesh=mesh,
        in_specs=(P(None, ("heads", "cells"), None), P(), P(), P(), P(("heads", "cells")), P()),
        out_specs=P(None, ("heads", "cells"), None),
        check_vma=False,
    )
```

```python
import math

import jax
import jax.numpy as jnp
from jax import lax
from jax.experimental import pallas as pl
from jax.experimental.pallas import tpu as pltpu
from jax.sharding import PartitionSpec as P

HEAD_DIM = 64
PAIR = 2 * HEAD_DIM
VAL_ROWS = PAIR + 16
ACC_ROWS = HEAD_DIM + 8
MASKED = -1e30
SCALE = 0.125 * math.log2(math.e)
COLS = 256
ROWS, LANES = 16, 128
MORE = 1
BF16 = jnp.bfloat16
F32 = jnp.float32


def dot(a, b, a_dim=1, b_dim=0):
    return lax.dot_general(a, b, (((a_dim,), (b_dim,)), ((), ())), preferred_element_type=F32)


def one_hot(tags, count):
    lane = lax.broadcasted_iota(jnp.int32, tags.shape, 1).astype(F32)
    parts = [(tags == lane + start).astype(F32) for start in range(0, count, LANES)]
    return jnp.concatenate(parts, axis=1).astype(BF16)


def pack_kernel(order, x_hbm, gain_hbm, tile_hbm, *refs):
    out_refs, (cells_ref, gain_ref, tile_ref, sems) = refs[: len(order)], refs[len(order) :]
    genes, rows, width = cells_ref.shape
    gene = lax.rem(lax.axis_index("cells"), genes)
    moves = [(gain_hbm, gain_ref), (tile_hbm, tile_ref)]
    moves += [(x_hbm.at[gene ^ k], cells_ref.at[i]) for i, k in enumerate(order)]
    copies = [pltpu.make_async_copy(*move, sems.at[i]) for i, move in enumerate(moves)]
    for copy in copies:
        copy.start()
    for copy in copies:
        copy.wait()
    gain = gain_ref[...]
    row = lax.broadcasted_iota(jnp.int32, (rows, rows), 0)
    column = lax.broadcasted_iota(jnp.int32, (rows, rows), 1)
    tiles = jnp.where(row == column, tile_ref[...].astype(F32), 0.0)
    tags = jnp.sum(tiles, axis=1, keepdims=True)
    parts = rows // ROWS
    lane = lax.broadcasted_iota(jnp.int32, (ROWS, LANES), 1) // (LANES // parts)
    tag_tile = jnp.zeros((ROWS, LANES), F32)
    for part in range(parts):
        tag_tile = jnp.where(lane == part, tags[part * ROWS : (part + 1) * ROWS], tag_tile)
    for i in range(genes):
        x32 = cells_ref[i].astype(F32)
        mean = jnp.mean(x32 * x32, axis=-1, keepdims=True)
        normed = (x32 * lax.rsqrt(mean + 1e-05) * gain).astype(BF16)
        place = 0
        for row in range(0, rows, ROWS):
            for start in range(0, width, LANES):
                tile = normed[row : row + ROWS, start : start + LANES]
                out_refs[i][place : place + ROWS, :] = tile
                place += ROWS
        out_refs[i][place:, :] = tag_tile.astype(BF16)


def pack(cells_in, gain, tiles, order):
    genes, rows, width = cells_in.shape
    operands = [cells_in, gain.reshape(1, width), tiles.reshape(1, rows)]
    operands = [pltpu.with_memory_space_constraint(value, pltpu.HBM) for value in operands]
    return pl.pallas_call(
        lambda *refs: pack_kernel(order, *refs),
        out_shape=[jax.ShapeDtypeStruct((rows * width // LANES + ROWS, LANES), BF16)] * genes,
        in_specs=[pl.BlockSpec(memory_space=pltpu.HBM)] * 3,
        out_specs=[pl.BlockSpec(memory_space=pltpu.VMEM)] * genes,
        scratch_shapes=[
            pltpu.VMEM(cells_in.shape, BF16),
            pltpu.VMEM((1, width), F32),
            pltpu.VMEM((1, rows), jnp.int32),
            pltpu.SemaphoreType.DMA((genes + 2,)),
        ],
        compiler_params=pltpu.CompilerParams(vmem_limit_bytes=4 * 1024 * 1024),
        name="pack",
    )(*operands)


def unpack_kernel(order, *refs):
    piece_refs, (out_hbm, sems) = refs[: len(order)], refs[len(order) :]
    gene = lax.rem(lax.axis_index("cells"), len(order))
    copies = []
    for i, (k, piece_ref) in enumerate(zip(order, piece_refs)):
        copies.append(pltpu.make_async_copy(piece_ref, out_hbm.at[gene ^ k], sems.at[i]))
        copies[-1].start()
    for copy in copies:
        copy.wait()


def unpack(pieces, order, shape):
    return pl.pallas_call(
        lambda *refs: unpack_kernel(order, *refs),
        out_shape=jax.ShapeDtypeStruct(shape, BF16),
        in_specs=[pl.BlockSpec(memory_space=pl.ANY)] * len(order),
        out_specs=pl.BlockSpec(memory_space=pltpu.HBM),
        scratch_shapes=[pltpu.SemaphoreType.DMA((len(order),))],
        compiler_params=pltpu.CompilerParams(vmem_limit_bytes=1024 * 1024),
        name="unpack",
    )(*pieces)


class Stage:
    def __init__(self, env, pieces, queries, blocks, attend, fetch=False, finish=False, keep=()):
        self.pieces, self.queries, self.blocks = pieces, queries, blocks
        self.attend, self.fetch, self.finish, self.keep = attend, fetch, finish, keep
        self.width = env["w_hbm"].shape[0]
        self.piece = env["piece"]
        self.tiles = env["adjacency_hbm"].shape[0]
        self.pairs = self.width // PAIR
        self.rows = {q: sum(size for _, _, size in pieces["q", q]) for q in {q for q, _ in attend}}
        self.cells = {b: sum(size for _, _, size in pieces["k", b]) for b in {b for _, b in attend}}
        self.block = max(self.cells.values())
        self.touched = sorted({q for q, _ in attend})
        ins = {"w_hbm", "adjacency_hbm"} if fetch else {"w"}
        if queries and not fetch:
            ins.add("adjacency")
        for group in [("q", q) for q in queries] + [("k", b) for b in {b for _, b in attend}]:
            ins |= {name for name, _, _ in pieces[group]}
        for q in self.touched:
            if q not in queries:
                ins |= {f"Q{q}", f"G{q}"}
            if f"acc{q}" in env:
                ins |= {f"acc{q}", f"top{q}"}
        for b in {b for _, b in attend} - set(blocks):
            ins |= {f"K{b}", f"V{b}"}
        if finish:
            ins.add("w_out")
        self.ins = sorted(ins)
        self.held = set(ins)
        shapes = {}
        for q in queries:
            shapes[f"Q{q}"] = ((self.pairs, 2 * self.rows[q], PAIR), BF16)
            shapes[f"G{q}"] = ((self.tiles, 2 * self.rows[q]), BF16)
        for q in self.touched:
            shapes[f"acc{q}"] = ((self.pairs, ACC_ROWS, 2 * self.rows[q]), F32)
            shapes[f"top{q}"] = ((self.pairs, 2 * self.rows[q]), F32)
        for b in blocks:
            shapes[f"K{b}"] = ((self.cells[b], self.width), BF16)
            shapes[f"V{b}"] = ((self.pairs, VAL_ROWS, self.cells[b]), BF16)
        outs, scratch = {}, {}
        for name, shape in shapes.items():
            stays = name[0] in "KV" and int(name[1:]) not in keep
            (scratch if finish or stays else outs)[name] = shape
        if finish:
            for q in self.touched:
                outs[f"out{q}"] = ((self.rows[q], self.width), BF16)
        self.outs, self.scratch = outs, scratch

    def body(self, *refs):
        count = len(self.ins)
        names = list(self.outs) + ["adjacency", "w"] * self.fetch + list(self.scratch)
        more = ["cells", "bias", "weights"] + ["attended"] * self.finish
        more += ["pairs_allowed", "sems"] * self.fetch
        self.read = dict(zip(self.ins, refs[:count]))
        self.write = dict(zip(names + more, refs[count:]))
        self.w = self.write["w"] if self.fetch else self.read["w"]
        if self.fetch:
            self.start_copies()
        if self.fetch:
            self.copies[0].wait()
        for q in self.queries:
            self.project_queries(q)
        if self.fetch:
            self.copies[1].wait()
        for b in self.blocks:
            cells = self.load_cells("k", b)
            self.project_keys(b, cells)
            if not self.fetch:
                self.project_values(b, cells)
        self.attend_all()
        if self.finish:
            for q in self.touched:
                self.project_out(q)

    def ref(self, name):
        return self.write[name] if name in self.write else self.read[name]

    def tiles_of(self, kind, index):
        per = self.piece * self.width // LANES + ROWS
        for name, start, size in self.pieces[kind, index]:
            for piece in range(start // self.piece, (start + size) // self.piece):
                yield self.read[name], piece * per

    def start_copies(self):
        width, sems = self.width, self.write["sems"]
        moves = [(self.read["adjacency_hbm"], self.write["pairs_allowed"])]
        for start in (0, width, 2 * width):
            part = slice(start, start + width)
            moves.append((self.read["w_hbm"].at[:, part], self.write["w"].at[:, part]))
        copies = [pltpu.make_async_copy(*move, sems.at[i]) for i, move in enumerate(moves)]
        for copy in copies:
            copy.start()
        copies[0].wait()
        self.copies = copies[1:]
        allowed = self.write["pairs_allowed"][...]
        self.write["adjacency"][...] = allowed.astype(F32).astype(BF16)

    def load_cells(self, kind, index):
        cells_ref, row = self.write["cells"], 0
        for ref, place in self.tiles_of(kind, index):
            for _ in range(self.piece // ROWS):
                for start in range(0, self.width, LANES):
                    cells_ref[row : row + ROWS, start : start + LANES] = ref[place : place + ROWS, :]
                    place += ROWS
                row += ROWS
        return cells_ref[:row, :]

    def tags_of(self, kind, index):
        tags, parts = [], self.piece // ROWS
        for ref, place in self.tiles_of(kind, index):
            place += self.piece * self.width // LANES
            tile = ref[place : place + ROWS, :].astype(F32)
            for part in range(parts):
                column = part * (LANES // parts)
                tags.append(jnp.broadcast_to(tile[:, column : column + 1], tile.shape))
        return one_hot(jnp.concatenate(tags, axis=0), self.tiles)

    def project_queries(self, q):
        rows = self.rows[q]
        cells = self.load_cells("q", q)
        for start in range(0, self.width, COLS):
            query = (dot(cells, self.w[:, start : start + COLS]) * SCALE).astype(BF16)
            lane = lax.broadcasted_iota(jnp.int32, (rows, PAIR), 1)
            for part in range(COLS // PAIR):
                both = query[:, part * PAIR : (part + 1) * PAIR]
                pair = start // PAIR + part
                none = jnp.zeros_like(both)
                self.write[f"Q{q}"][pair, :rows, :] = jnp.where(lane < HEAD_DIM, both, none)
                self.write[f"Q{q}"][pair, rows:, :] = jnp.where(lane < HEAD_DIM, none, both)
        near = dot(self.ref("adjacency")[...], self.tags_of("q", q), 1, 1)
        near = ((1.0 - near) * MASKED).astype(BF16)
        self.write[f"G{q}"][...] = jnp.concatenate([near, near], axis=1)

    def project_keys(self, b, cells):
        for start in range(0, self.width, COLS):
            part = slice(self.width + start, self.width + start + COLS)
            self.write[f"K{b}"][:, start : start + COLS] = dot(cells, self.w[:, part]).astype(BF16)

    def project_values(self, b, cells):
        ones = jnp.ones((self.pairs, VAL_ROWS - PAIR, self.cells[b]), BF16)
        self.write[f"V{b}"][:, PAIR:, :] = ones
        for start in range(0, self.width, COLS):
            part = slice(2 * self.width + start, 2 * self.width + start + COLS)
            values = dot(cells, self.w[:, part]).astype(BF16).T
            for i in range(COLS // PAIR):
                rows = values[i * PAIR : (i + 1) * PAIR]
                self.write[f"V{b}"][start // PAIR + i, :PAIR, :] = rows

    def attend_all(self):
        source = {q: self.read for q in self.touched if f"acc{q}" in self.held}
        before = None
        late = self.blocks if self.fetch else []
        for turn, (q, b) in enumerate(self.attend):
            after = self.start_turn(q, b, source.get(q), turn % 2)
            source[q] = self.write
            for pair in range(self.pairs):
                self.weigh(after, pair)
                if before is not None and late:
                    late = self.project_late_values(late)
                if before is not None:
                    self.add_values(before, pair)
            before = after
        if late:
            self.project_late_values(late)
        for pair in range(self.pairs):
            self.add_values(before, pair)

    def project_late_values(self, late):
        self.copies[2].wait()
        for b in late:
            self.project_values(b, self.load_cells("k", b))
        return []

    def start_turn(self, q, b, before, slot):
        cells = self.cells[b]
        bias_ref = self.write["bias"].at[slot, :cells]
        bias_ref[...] = dot(self.tags_of("k", b), self.ref(f"G{q}")[...])
        return (q, b, before, bias_ref, self.write["weights"].at[slot, :, :cells], {})

    def weigh(self, turn, pair):
        q, b, before, bias_ref, weight_ref, factors = turn
        keys = self.ref(f"K{b}")[:, pair * PAIR : (pair + 1) * PAIR]
        scores = dot(keys, self.ref(f"Q{q}")[pair], 1, 1) + bias_ref[...]
        top = jnp.max(scores, axis=0, keepdims=True)
        if before is not None:
            last = before[f"top{q}"][pair : pair + 1, :]
            top = jnp.maximum(top, last)
            factors[pair] = jnp.exp2(last - top)
        weight_ref[pair] = jnp.exp2(scores - top).astype(BF16)
        self.write[f"top{q}"][pair : pair + 1, :] = top

    def add_values(self, turn, pair):
        q, b, before, _, weight_ref, factors = turn
        half = self.rows[q]
        acc_ref = self.write[f"acc{q}"]
        summed = dot(self.ref(f"V{b}")[pair], weight_ref[pair])
        even, odd = summed[:HEAD_DIM, :half], summed[HEAD_DIM:PAIR, half:]
        both = jnp.concatenate([even, odd], axis=1)
        total = summed[PAIR : PAIR + ACC_ROWS - HEAD_DIM]
        if before is not None:
            both = both + before[f"acc{q}"][pair, :HEAD_DIM, :] * factors[pair]
            total = total + before[f"acc{q}"][pair, HEAD_DIM:, :] * factors[pair]
        acc_ref[pair, :HEAD_DIM, :] = both
        acc_ref[pair, HEAD_DIM:, :] = total

    def project_out(self, q):
        half = self.rows[q]
        acc_ref, att_ref = self.write[f"acc{q}"], self.write["attended"]
        for pair in range(self.pairs):
            total = acc_ref[pair, HEAD_DIM : HEAD_DIM + 1, :]
            part = (acc_ref[pair, :HEAD_DIM, :] / total).astype(BF16)
            row = pair * PAIR
            att_ref[row : row + HEAD_DIM, :] = part[:, :half]
            att_ref[row + HEAD_DIM : row + PAIR, :] = part[:, half:]
        attended = att_ref[...].T
        for start in range(0, self.width, COLS):
            out = dot(attended, self.read["w_out"][:, start : start + COLS]).astype(BF16)
            self.write[f"out{q}"][:, start : start + COLS] = out

    def call(self, env, name):
        vmem = pl.BlockSpec(memory_space=pltpu.VMEM)
        hbm = pl.BlockSpec(memory_space=pltpu.HBM)
        operands = [env[n] for n in self.ins]
        out_shape = [jax.ShapeDtypeStruct(*shape) for shape in self.outs.values()]
        out_specs = [vmem] * len(out_shape)
        rows = max(self.rows.values())
        scratch = [pltpu.VMEM(*shape) for shape in self.scratch.values()]
        scratch += [
            pltpu.VMEM((max(self.block, rows), self.width), BF16),
            pltpu.VMEM((2, self.block, 2 * rows), F32),
            pltpu.VMEM((2, self.pairs, self.block, 2 * rows), BF16),
        ]
        if self.finish:
            scratch.append(pltpu.VMEM((self.width, rows), BF16))
        if self.fetch:
            shape = (self.width, 3 * self.width)
            out_shape += [jax.ShapeDtypeStruct((self.tiles, self.tiles), BF16), pltpu.VMEM(shape, BF16)]
            out_specs += [vmem, vmem]
            scratch += [
                pltpu.VMEM((self.tiles, self.tiles), jnp.int32),
                pltpu.SemaphoreType.DMA((4,)),
            ]
        flops = 2 * self.width * (
            2 * sum(self.cells[b] for b in self.blocks) * self.width
            + (len(self.queries) + self.finish * len(self.touched)) * rows * self.width
            + 8 * sum(self.cells[b] for _, b in self.attend) * rows
        )
        outs = pl.pallas_call(
            self.body,
            out_shape=tuple(out_shape),
            in_specs=[hbm if n.endswith("_hbm") else vmem for n in self.ins],
            out_specs=tuple(out_specs),
            scratch_shapes=scratch,
            compiler_params=pltpu.CompilerParams(vmem_limit_bytes=16 * 1024 * 1024),
            cost_estimate=pl.CostEstimate(flops=flops, bytes_accessed=1 << 23, transcendentals=0),
            name=name,
        )(*operands)
        env.update(zip(list(self.outs) + ["adjacency", "w"] * self.fetch, outs))


def on_device(cells_in, gain, w_qkv, w_out, tile_of_cell, tile_adjacent):
    genes, cell_dev, width = cells_in.shape
    head_devs, cell_devs = lax.axis_size("heads"), lax.axis_size("cells")
    sets = cell_devs // genes
    half = genes // 2
    same = [[s * genes + g for s in range(sets)] for g in range(genes)]

    def over_cells(value, step):
        return lax.ppermute(value, "cells", [(i, i ^ step) for i in range(cell_devs)])

    def over_heads(value, step):
        return lax.ppermute(value, "heads", [(i, i ^ step) for i in range(head_devs)])

    order = [4, 1, 3, 0, 2, 6, 5, 7] if genes == 8 else list(range(genes))
    back = [0, 4, 1, 2, 6, 5, 7, 3] if genes == 8 else order
    packed = pack(cells_in, gain, tile_of_cell, order)
    arrived = [over_cells(piece, k) if k else piece for piece, k in zip(packed, order)]
    env = {"w_out": w_out, "piece": cell_dev}
    held = {"w_hbm": w_qkv, "adjacency_hbm": tile_adjacent}
    for name, value in held.items():
        env[name] = pltpu.with_memory_space_constraint(value, pltpu.HBM)
    pieces = {}
    rows = half * cell_dev

    def spread(group, own, beside):
        env[f"own{group}"] = own
        held = own
        if sets > 1:
            held = lax.all_gather(own, "cells", axis=0, axis_index_groups=same, tiled=True)
        for step in range(0, head_devs, 2):
            env[f"chunk{group}{step}"] = over_heads(held, step) if step else held
            if step in beside:
                env[f"beside{group}{step}"] = over_heads(env[f"chunk{group}{step}"], 1)

    shallow = sets == 1 and head_devs == 4
    cut = half + MORE if shallow else half
    first = jnp.concatenate(arrived[:cut], 0)
    more = (cut - half) * cell_dev
    pieces["q", 0] = [("own0", 0, rows)]
    pieces["q", 1] = [("own0", rows, more)] * (more > 0) + [("own1", 0, rows - more)]
    steps = range(0, head_devs, 2)
    spread(0, first, steps)
    if shallow:
        def env_rows(name):
            return rows + (more if "0" == name.lstrip("ownchunkbeside")[0] else -more)

        blocks = [["own0"], ["beside00", "own1"], ["beside10", "chunk02"], ["beside02", "chunk12"], ["beside12"]]
        for b, names in enumerate(blocks):
            pieces["k", b] = [(name, 0, env_rows(name)) for name in names]
        Stage(env, pieces, [0], [0], [(0, 0)], fetch=True, keep=[0]).call(env, "first_group")
        env["w"], *late = lax.optimization_barrier((env["w"], *arrived[cut:]))
        spread(1, jnp.concatenate(late, 0), [0])
        attend = [(0, 1), (1, 0), (1, 1), (0, 2), (1, 2)]
        Stage(env, pieces, [1], [1, 2], attend).call(env, "second_group")
        env["chunk12"], env["top1"] = lax.optimization_barrier((env["chunk12"], env["top1"]))
        env["beside12"] = over_heads(env["chunk12"], 1)
        Stage(env, pieces, [], [3], [(0, 3), (1, 3)]).call(env, "far")
        Stage(env, pieces, [], [4], [(0, 4), (1, 4)], finish=True).call(env, "last")
    else:
        spread(1, jnp.concatenate(arrived[half:], 0), steps)
        names = [f"{kind}{group}{step}" for group in range(2) for step in steps for kind in ("chunk", "beside")]
        for b, (name, s) in enumerate((name, s) for name in names for s in range(sets)):
            pieces["k", b] = [(name, s * rows, rows)]
        last = len(names) * sets - 1
        for b in range(last + 1):
            attend = [(0, b), (1, b)]
            stage = Stage(env, pieces, [] if b else [0, 1], [b], attend, fetch=b == 0, finish=b == last)
            stage.call(env, f"block_{b}")
    returned = []
    for k in back:
        place = order.index(k)
        start = place % half * cell_dev
        piece = env[f"out{place // half}"][start : start + cell_dev]
        returned.append(over_cells(piece, k) if k else piece)
    return unpack(returned, back, cells_in.shape)


def solution(mesh):
    return jax.shard_map(
        on_device,
        mesh=mesh,
        in_specs=(P(None, ("heads", "cells"), None), P(), P(), P(), P(("heads", "cells")), P()),
        out_specs=P(None, ("heads", "cells"), None),
        check_vma=False,
    )
```

```python
import math

import jax
import jax.numpy as jnp
from jax import lax
from jax.experimental import pallas as pl
from jax.experimental.pallas import tpu as pltpu
from jax.sharding import PartitionSpec as P

HEAD_DIM = 64
PAIR = 2 * HEAD_DIM
VAL_ROWS = PAIR + 16
ACC_ROWS = HEAD_DIM + 8
MASKED = -1e30
SCALE = 0.125 * math.log2(math.e)
COLS = 256
ROWS, LANES = 16, 128
MORE = 1
BF16 = jnp.bfloat16
F32 = jnp.float32


def dot(a, b, a_dim=1, b_dim=0):
    return lax.dot_general(a, b, (((a_dim,), (b_dim,)), ((), ())), preferred_element_type=F32)


def one_hot(tags, count):
    lane = lax.broadcasted_iota(jnp.int32, tags.shape, 1).astype(F32)
    parts = [(tags == lane + start).astype(F32) for start in range(0, count, LANES)]
    return jnp.concatenate(parts, axis=1).astype(BF16)


def pack_kernel(order, x_hbm, gain_hbm, tile_hbm, *refs):
    out_refs, (cells_ref, gain_ref, tile_ref, sems) = refs[: len(order)], refs[len(order) :]
    genes, rows, width = cells_ref.shape
    gene = lax.rem(lax.axis_index("cells"), genes)
    moves = [(gain_hbm, gain_ref), (tile_hbm, tile_ref)]
    moves += [(x_hbm.at[gene ^ k], cells_ref.at[i]) for i, k in enumerate(order)]
    copies = [pltpu.make_async_copy(*move, sems.at[i]) for i, move in enumerate(moves)]
    for copy in copies:
        copy.start()
    for copy in copies:
        copy.wait()
    gain = gain_ref[...]
    row = lax.broadcasted_iota(jnp.int32, (rows, rows), 0)
    column = lax.broadcasted_iota(jnp.int32, (rows, rows), 1)
    tiles = jnp.where(row == column, tile_ref[...].astype(F32), 0.0)
    tags = jnp.sum(tiles, axis=1, keepdims=True)
    parts = rows // ROWS
    lane = lax.broadcasted_iota(jnp.int32, (ROWS, LANES), 1) // (LANES // parts)
    tag_tile = jnp.zeros((ROWS, LANES), F32)
    for part in range(parts):
        tag_tile = jnp.where(lane == part, tags[part * ROWS : (part + 1) * ROWS], tag_tile)
    for i in range(genes):
        x32 = cells_ref[i].astype(F32)
        mean = jnp.mean(x32 * x32, axis=-1, keepdims=True)
        normed = (x32 * lax.rsqrt(mean + 1e-05) * gain).astype(BF16)
        place = 0
        for row in range(0, rows, ROWS):
            for start in range(0, width, LANES):
                tile = normed[row : row + ROWS, start : start + LANES]
                out_refs[i][place : place + ROWS, :] = tile
                place += ROWS
        out_refs[i][place:, :] = tag_tile.astype(BF16)


def pack(cells_in, gain, tiles, order):
    genes, rows, width = cells_in.shape
    operands = [cells_in, gain.reshape(1, width), tiles.reshape(1, rows)]
    operands = [pltpu.with_memory_space_constraint(value, pltpu.HBM) for value in operands]
    return pl.pallas_call(
        lambda *refs: pack_kernel(order, *refs),
        out_shape=[jax.ShapeDtypeStruct((rows * width // LANES + ROWS, LANES), BF16)] * genes,
        in_specs=[pl.BlockSpec(memory_space=pltpu.HBM)] * 3,
        out_specs=[pl.BlockSpec(memory_space=pltpu.VMEM)] * genes,
        scratch_shapes=[
            pltpu.VMEM(cells_in.shape, BF16),
            pltpu.VMEM((1, width), F32),
            pltpu.VMEM((1, rows), jnp.int32),
            pltpu.SemaphoreType.DMA((genes + 2,)),
        ],
        compiler_params=pltpu.CompilerParams(vmem_limit_bytes=4 * 1024 * 1024),
        name="pack",
    )(*operands)


def unpack_kernel(order, *refs):
    piece_refs, (out_hbm, sems) = refs[: len(order)], refs[len(order) :]
    gene = lax.rem(lax.axis_index("cells"), len(order))
    copies = []
    for i, (k, piece_ref) in enumerate(zip(order, piece_refs)):
        copies.append(pltpu.make_async_copy(piece_ref, out_hbm.at[gene ^ k], sems.at[i]))
        copies[-1].start()
    for copy in copies:
        copy.wait()


def unpack(pieces, order, shape):
    return pl.pallas_call(
        lambda *refs: unpack_kernel(order, *refs),
        out_shape=jax.ShapeDtypeStruct(shape, BF16),
        in_specs=[pl.BlockSpec(memory_space=pl.ANY)] * len(order),
        out_specs=pl.BlockSpec(memory_space=pltpu.HBM),
        scratch_shapes=[pltpu.SemaphoreType.DMA((len(order),))],
        compiler_params=pltpu.CompilerParams(vmem_limit_bytes=1024 * 1024),
        name="unpack",
    )(*pieces)


class Stage:
    def __init__(self, env, pieces, queries, blocks, attend, fetch=False, finish=False, keep=()):
        self.pieces, self.queries, self.blocks = pieces, queries, blocks
        self.attend, self.fetch, self.finish, self.keep = attend, fetch, finish, keep
        self.width = env["w_hbm"].shape[0]
        self.piece = env["piece"]
        self.tiles = env["adjacency_hbm"].shape[0]
        self.pairs = self.width // PAIR
        self.rows = {q: sum(size for _, _, size in pieces["q", q]) for q in {q for q, _ in attend}}
        self.cells = {b: sum(size for _, _, size in pieces["k", b]) for b in {b for _, b in attend}}
        self.block = max(self.cells.values())
        self.touched = sorted({q for q, _ in attend})
        ins = {"w_hbm", "adjacency_hbm"} if fetch else {"w"}
        if queries and not fetch:
            ins.add("adjacency")
        for group in [("q", q) for q in queries] + [("k", b) for b in {b for _, b in attend}]:
            ins |= {name for name, _, _ in pieces[group]}
        for q in self.touched:
            if q not in queries:
                ins |= {f"Q{q}", f"G{q}"}
            if f"acc{q}" in env:
                ins |= {f"acc{q}", f"top{q}"}
        for b in {b for _, b in attend} - set(blocks):
            ins |= {f"K{b}", f"V{b}"}
        if finish:
            ins.add("w_out")
        self.ins = sorted(ins)
        self.held = set(ins)
        shapes = {}
        for q in queries:
            shapes[f"Q{q}"] = ((self.pairs, 2 * self.rows[q], PAIR), BF16)
            shapes[f"G{q}"] = ((self.tiles, 2 * self.rows[q]), BF16)
        for q in self.touched:
            shapes[f"acc{q}"] = ((self.pairs, ACC_ROWS, 2 * self.rows[q]), F32)
            shapes[f"top{q}"] = ((self.pairs, 2 * self.rows[q]), F32)
        for b in blocks:
            shapes[f"K{b}"] = ((self.cells[b], self.width), BF16)
            shapes[f"V{b}"] = ((self.pairs, VAL_ROWS, self.cells[b]), BF16)
        outs, scratch = {}, {}
        for name, shape in shapes.items():
            stays = name[0] in "KV" and int(name[1:]) not in keep
            (scratch if finish or stays else outs)[name] = shape
        if finish:
            for q in self.touched:
                outs[f"out{q}"] = ((self.rows[q], self.width), BF16)
        self.outs, self.scratch = outs, scratch

    def body(self, *refs):
        count = len(self.ins)
        names = list(self.outs) + ["adjacency", "w"] * self.fetch + list(self.scratch)
        more = ["cells", "bias", "weights"] + ["attended"] * self.finish
        more += ["pairs_allowed", "sems"] * self.fetch
        self.read = dict(zip(self.ins, refs[:count]))
        self.write = dict(zip(names + more, refs[count:]))
        self.w = self.write["w"] if self.fetch else self.read["w"]
        if self.fetch:
            self.start_copies()
        if self.fetch:
            self.copies[0].wait()
        for q in self.queries:
            self.project_queries(q)
        self.late = self.fetch and len(self.attend) == 1
        if self.fetch:
            self.copies[1].wait()
            if not self.late:
                self.copies[2].wait()
        self.plan()
        self.attend_all()
        if self.finish:
            for q in self.touched:
                self.project_out(q)

    def ref(self, name):
        return self.write[name] if name in self.write else self.read[name]

    def tiles_of(self, kind, index):
        per = self.piece * self.width // LANES + ROWS
        for name, start, size in self.pieces[kind, index]:
            for piece in range(start // self.piece, (start + size) // self.piece):
                yield self.read[name], piece * per

    def start_copies(self):
        width, sems = self.width, self.write["sems"]
        moves = [(self.read["adjacency_hbm"], self.write["pairs_allowed"])]
        for start in (0, width, 2 * width):
            part = slice(start, start + width)
            moves.append((self.read["w_hbm"].at[:, part], self.write["w"].at[:, part]))
        copies = [pltpu.make_async_copy(*move, sems.at[i]) for i, move in enumerate(moves)]
        for copy in copies:
            copy.start()
        copies[0].wait()
        self.copies = copies[1:]
        allowed = self.write["pairs_allowed"][...]
        self.write["adjacency"][...] = allowed.astype(F32).astype(BF16)

    def load_cells(self, kind, index, slot=0):
        cells_ref, row = self.write["cells"].at[slot], 0
        for ref, place in self.tiles_of(kind, index):
            for _ in range(self.piece // ROWS):
                for start in range(0, self.width, LANES):
                    cells_ref[row : row + ROWS, start : start + LANES] = ref[place : place + ROWS, :]
                    place += ROWS
                row += ROWS
        return lambda: cells_ref[:row, :]

    def tags_of(self, kind, index):
        tags, parts = [], self.piece // ROWS
        for ref, place in self.tiles_of(kind, index):
            place += self.piece * self.width // LANES
            tile = ref[place : place + ROWS, :].astype(F32)
            for part in range(parts):
                column = part * (LANES // parts)
                tags.append(jnp.broadcast_to(tile[:, column : column + 1], tile.shape))
        return one_hot(jnp.concatenate(tags, axis=0), self.tiles)

    def project_queries(self, q):
        rows = self.rows[q]
        cells = self.load_cells("q", q)()
        for start in range(0, self.width, COLS):
            query = (dot(cells, self.w[:, start : start + COLS]) * SCALE).astype(BF16)
            lane = lax.broadcasted_iota(jnp.int32, (rows, PAIR), 1)
            for part in range(COLS // PAIR):
                both = query[:, part * PAIR : (part + 1) * PAIR]
                pair = start // PAIR + part
                none = jnp.zeros_like(both)
                self.write[f"Q{q}"][pair, :rows, :] = jnp.where(lane < HEAD_DIM, both, none)
                self.write[f"Q{q}"][pair, rows:, :] = jnp.where(lane < HEAD_DIM, none, both)
        near = dot(self.ref("adjacency")[...], self.tags_of("q", q), 1, 1)
        near = ((1.0 - near) * MASKED).astype(BF16)
        self.write[f"G{q}"][...] = jnp.concatenate([near, near], axis=1)

    def plan(self):
        self.due = {}
        order = [b for _, b in self.attend]
        for b in self.blocks:
            turn = order.index(b)
            cells = self.load_cells("k", b, self.blocks.index(b))
            for start in range(0, self.width, COLS):
                self.due.setdefault(turn, []).append((self.project_keys, b, cells, start))
                self.due.setdefault(turn + 1, []).append((self.project_values, b, cells, start))

    def run_due(self, turn, step=0, steps=1):
        tasks = self.due.get(turn, [])
        for task, *operands in tasks[len(tasks) * step // steps : len(tasks) * (step + 1) // steps]:
            task(*operands)

    def project_keys(self, b, cells, start):
        part = slice(self.width + start, self.width + start + COLS)
        self.write[f"K{b}"][:, start : start + COLS] = dot(cells(), self.w[:, part]).astype(BF16)

    def project_values(self, b, cells, start):
        part = slice(2 * self.width + start, 2 * self.width + start + COLS)
        values = dot(cells(), self.w[:, part]).astype(BF16).T
        for i in range(COLS // PAIR):
            pair = start // PAIR + i
            self.write[f"V{b}"][pair, :PAIR, :] = values[i * PAIR : (i + 1) * PAIR]
            ones = jnp.ones((VAL_ROWS - PAIR, self.cells[b]), BF16)
            self.write[f"V{b}"][pair, PAIR:, :] = ones

    def attend_all(self):
        source = {q: self.read for q in self.touched if f"acc{q}" in self.held}
        before = None
        self.run_due(0)
        for turn, (q, b) in enumerate(self.attend):
            after = self.start_turn(q, b, source.get(q), turn % 2)
            source[q] = self.write
            for pair in range(self.pairs):
                self.weigh(after, pair)
                if not self.late:
                    self.run_due(turn + 1, pair, self.pairs)
                if before is not None:
                    self.add_values(before, pair)
            before = after
        if self.late:
            self.copies[2].wait()
            self.run_due(len(self.attend))
        for pair in range(self.pairs):
            self.add_values(before, pair)

    def start_turn(self, q, b, before, slot):
        cells = self.cells[b]
        bias_ref = self.write["bias"].at[slot, :cells]
        bias_ref[...] = dot(self.tags_of("k", b), self.ref(f"G{q}")[...])
        return (q, b, before, bias_ref, self.write["weights"].at[slot, :, :cells], {})

    def weigh(self, turn, pair):
        q, b, before, bias_ref, weight_ref, factors = turn
        keys = self.ref(f"K{b}")[:, pair * PAIR : (pair + 1) * PAIR]
        scores = dot(keys, self.ref(f"Q{q}")[pair], 1, 1) + bias_ref[...]
        top = jnp.max(scores, axis=0, keepdims=True)
        if before is not None:
            last = before[f"top{q}"][pair : pair + 1, :]
            top = jnp.maximum(top, last)
            factors[pair] = jnp.exp2(last - top)
        weight_ref[pair] = jnp.exp2(scores - top).astype(BF16)
        self.write[f"top{q}"][pair : pair + 1, :] = top

    def add_values(self, turn, pair):
        q, b, before, _, weight_ref, factors = turn
        half = self.rows[q]
        acc_ref = self.write[f"acc{q}"]
        summed = dot(self.ref(f"V{b}")[pair], weight_ref[pair])
        even, odd = summed[:HEAD_DIM, :half], summed[HEAD_DIM:PAIR, half:]
        both = jnp.concatenate([even, odd], axis=1)
        total = summed[PAIR : PAIR + ACC_ROWS - HEAD_DIM]
        if before is not None:
            both = both + before[f"acc{q}"][pair, :HEAD_DIM, :] * factors[pair]
            total = total + before[f"acc{q}"][pair, HEAD_DIM:, :] * factors[pair]
        acc_ref[pair, :HEAD_DIM, :] = both
        acc_ref[pair, HEAD_DIM:, :] = total

    def project_out(self, q):
        half = self.rows[q]
        acc_ref, att_ref = self.write[f"acc{q}"], self.write["attended"]
        for pair in range(self.pairs):
            total = acc_ref[pair, HEAD_DIM : HEAD_DIM + 1, :]
            part = (acc_ref[pair, :HEAD_DIM, :] / total).astype(BF16)
            row = pair * PAIR
            att_ref[row : row + HEAD_DIM, :] = part[:, :half]
            att_ref[row + HEAD_DIM : row + PAIR, :] = part[:, half:]
        attended = att_ref[...].T
        for start in range(0, self.width, COLS):
            out = dot(attended, self.read["w_out"][:, start : start + COLS]).astype(BF16)
            self.write[f"out{q}"][:, start : start + COLS] = out

    def call(self, env, name):
        vmem = pl.BlockSpec(memory_space=pltpu.VMEM)
        hbm = pl.BlockSpec(memory_space=pltpu.HBM)
        operands = [env[n] for n in self.ins]
        out_shape = [jax.ShapeDtypeStruct(*shape) for shape in self.outs.values()]
        out_specs = [vmem] * len(out_shape)
        rows = max(self.rows.values())
        scratch = [pltpu.VMEM(*shape) for shape in self.scratch.values()]
        scratch += [
            pltpu.VMEM((max(len(self.blocks), 1), max(self.block, rows), self.width), BF16),
            pltpu.VMEM((2, self.block, 2 * rows), F32),
            pltpu.VMEM((2, self.pairs, self.block, 2 * rows), BF16),
        ]
        if self.finish:
            scratch.append(pltpu.VMEM((self.width, rows), BF16))
        if self.fetch:
            shape = (self.width, 3 * self.width)
            out_shape += [jax.ShapeDtypeStruct((self.tiles, self.tiles), BF16), pltpu.VMEM(shape, BF16)]
            out_specs += [vmem, vmem]
            scratch += [
                pltpu.VMEM((self.tiles, self.tiles), jnp.int32),
                pltpu.SemaphoreType.DMA((4,)),
            ]
        flops = 2 * self.width * (
            2 * sum(self.cells[b] for b in self.blocks) * self.width
            + (len(self.queries) + self.finish * len(self.touched)) * rows * self.width
            + 8 * sum(self.cells[b] for _, b in self.attend) * rows
        )
        outs = pl.pallas_call(
            self.body,
            out_shape=tuple(out_shape),
            in_specs=[hbm if n.endswith("_hbm") else vmem for n in self.ins],
            out_specs=tuple(out_specs),
            scratch_shapes=scratch,
            compiler_params=pltpu.CompilerParams(vmem_limit_bytes=16 * 1024 * 1024),
            cost_estimate=pl.CostEstimate(flops=flops, bytes_accessed=1 << 23, transcendentals=0),
            name=name,
        )(*operands)
        env.update(zip(list(self.outs) + ["adjacency", "w"] * self.fetch, outs))


def on_device(cells_in, gain, w_qkv, w_out, tile_of_cell, tile_adjacent):
    genes, cell_dev, width = cells_in.shape
    head_devs, cell_devs = lax.axis_size("heads"), lax.axis_size("cells")
    sets = cell_devs // genes
    half = genes // 2
    same = [[s * genes + g for s in range(sets)] for g in range(genes)]

    def over_cells(value, step):
        return lax.ppermute(value, "cells", [(i, i ^ step) for i in range(cell_devs)])

    def over_heads(value, step):
        return lax.ppermute(value, "heads", [(i, i ^ step) for i in range(head_devs)])

    order = [4, 1, 3, 0, 2, 6, 5, 7] if genes == 8 else list(range(genes))
    back = [0, 4, 1, 2, 6, 5, 7, 3] if genes == 8 else order
    packed = pack(cells_in, gain, tile_of_cell, order)
    arrived = [over_cells(piece, k) if k else piece for piece, k in zip(packed, order)]
    env = {"w_out": w_out, "piece": cell_dev}
    held = {"w_hbm": w_qkv, "adjacency_hbm": tile_adjacent}
    for name, value in held.items():
        env[name] = pltpu.with_memory_space_constraint(value, pltpu.HBM)
    pieces = {}
    rows = half * cell_dev

    def spread(group, own, beside):
        env[f"own{group}"] = own
        held = own
        if sets > 1:
            held = lax.all_gather(own, "cells", axis=0, axis_index_groups=same, tiled=True)
        for step in range(0, head_devs, 2):
            env[f"chunk{group}{step}"] = over_heads(held, step) if step else held
            if step in beside:
                env[f"beside{group}{step}"] = over_heads(env[f"chunk{group}{step}"], 1)

    shallow = sets == 1 and head_devs == 4
    cut = half + MORE if shallow else half
    first = jnp.concatenate(arrived[:cut], 0)
    more = (cut - half) * cell_dev
    pieces["q", 0] = [("own0", 0, rows)]
    pieces["q", 1] = [("own0", rows, more)] * (more > 0) + [("own1", 0, rows - more)]
    steps = range(0, head_devs, 2)
    spread(0, first, steps)
    if shallow:
        def env_rows(name):
            return rows + (more if "0" == name.lstrip("ownchunkbeside")[0] else -more)

        blocks = [["own0"], ["beside00", "own1"], ["beside10", "chunk02"], ["beside02", "chunk12"], ["beside12"]]
        for b, names in enumerate(blocks):
            pieces["k", b] = [(name, 0, env_rows(name)) for name in names]
        Stage(env, pieces, [0], [0], [(0, 0)], fetch=True, keep=[0]).call(env, "first_group")
        env["w"], *late = lax.optimization_barrier((env["w"], *arrived[cut:]))
        spread(1, jnp.concatenate(late, 0), [0])
        attend = [(0, 1), (1, 0), (1, 1), (0, 2), (1, 2)]
        Stage(env, pieces, [1], [1, 2], attend).call(env, "second_group")
        env["chunk12"], env["top1"] = lax.optimization_barrier((env["chunk12"], env["top1"]))
        env["beside12"] = over_heads(env["chunk12"], 1)
        Stage(env, pieces, [], [3], [(0, 3), (1, 3)]).call(env, "far")
        Stage(env, pieces, [], [4], [(0, 4), (1, 4)], finish=True).call(env, "last")
    else:
        spread(1, jnp.concatenate(arrived[half:], 0), steps)
        names = [f"{kind}{group}{step}" for group in range(2) for step in steps for kind in ("chunk", "beside")]
        for b, (name, s) in enumerate((name, s) for name in names for s in range(sets)):
            pieces["k", b] = [(name, s * rows, rows)]
        last = len(names) * sets - 1
        for b in range(last + 1):
            attend = [(0, b), (1, b)]
            stage = Stage(env, pieces, [] if b else [0, 1], [b], attend, fetch=b == 0, finish=b == last)
            stage.call(env, f"block_{b}")
    returned = []
    for k in back:
        place = order.index(k)
        start = place % half * cell_dev
        piece = env[f"out{place // half}"][start : start + cell_dev]
        returned.append(over_cells(piece, k) if k else piece)
    return unpack(returned, back, cells_in.shape)


def solution(mesh):
    return jax.shard_map(
        on_device,
        mesh=mesh,
        in_specs=(P(None, ("heads", "cells"), None), P(), P(), P(), P(("heads", "cells")), P()),
        out_specs=P(None, ("heads", "cells"), None),
        check_vma=False,
    )
```

```python
import math

import jax
import jax.numpy as jnp
from jax import lax
from jax.experimental import pallas as pl
from jax.experimental.pallas import tpu as pltpu
from jax.sharding import PartitionSpec as P

HEAD_DIM = 64
PAIR = 2 * HEAD_DIM
VAL_ROWS = PAIR + 16
ACC_ROWS = HEAD_DIM + 8
MASKED = -1e30
LOWEST_TOP = -1e29
SCALE = 0.125 * math.log2(math.e)
COLS = 256
ROWS, LANES = 16, 128
MORE = 1
BF16 = jnp.bfloat16
F32 = jnp.float32


def dot(a, b, a_dim=1, b_dim=0):
    return lax.dot_general(a, b, (((a_dim,), (b_dim,)), ((), ())), preferred_element_type=F32)


def one_hot(tags, count):
    lane = lax.broadcasted_iota(jnp.int32, tags.shape, 1).astype(F32)
    parts = [(tags == lane + start).astype(F32) for start in range(0, count, LANES)]
    return jnp.concatenate(parts, axis=1).astype(BF16)


def pack_kernel(order, x_hbm, gain_hbm, tile_hbm, *refs):
    out_refs, (cells_ref, gain_ref, tile_ref, sems) = refs[: len(order)], refs[len(order) :]
    genes, rows, width = cells_ref.shape
    gene = lax.rem(lax.axis_index("cells"), genes)
    moves = [(gain_hbm, gain_ref), (tile_hbm, tile_ref)]
    moves += [(x_hbm.at[gene ^ k], cells_ref.at[i]) for i, k in enumerate(order)]
    copies = [pltpu.make_async_copy(*move, sems.at[i]) for i, move in enumerate(moves)]
    for copy in copies:
        copy.start()
    for copy in copies:
        copy.wait()
    gain = gain_ref[...]
    row = lax.broadcasted_iota(jnp.int32, (rows, rows), 0)
    column = lax.broadcasted_iota(jnp.int32, (rows, rows), 1)
    tiles = jnp.where(row == column, tile_ref[...].astype(F32), 0.0)
    tags = jnp.sum(tiles, axis=1, keepdims=True)
    parts = rows // ROWS
    lane = lax.broadcasted_iota(jnp.int32, (ROWS, LANES), 1) // (LANES // parts)
    tag_tile = jnp.zeros((ROWS, LANES), F32)
    for part in range(parts):
        tag_tile = jnp.where(lane == part, tags[part * ROWS : (part + 1) * ROWS], tag_tile)
    for i in range(genes):
        x32 = cells_ref[i].astype(F32)
        mean = jnp.mean(x32 * x32, axis=-1, keepdims=True)
        normed = (x32 * lax.rsqrt(mean + 1e-05) * gain).astype(BF16)
        place = 0
        for row in range(0, rows, ROWS):
            for start in range(0, width, LANES):
                tile = normed[row : row + ROWS, start : start + LANES]
                out_refs[i][place : place + ROWS, :] = tile
                place += ROWS
        out_refs[i][place:, :] = tag_tile.astype(BF16)


def pack(cells_in, gain, tiles, order):
    genes, rows, width = cells_in.shape
    operands = [cells_in, gain.reshape(1, width), tiles.reshape(1, rows)]
    operands = [pltpu.with_memory_space_constraint(value, pltpu.HBM) for value in operands]
    return pl.pallas_call(
        lambda *refs: pack_kernel(order, *refs),
        out_shape=[jax.ShapeDtypeStruct((rows * width // LANES + ROWS, LANES), BF16)] * genes,
        in_specs=[pl.BlockSpec(memory_space=pltpu.HBM)] * 3,
        out_specs=[pl.BlockSpec(memory_space=pltpu.VMEM)] * genes,
        scratch_shapes=[
            pltpu.VMEM(cells_in.shape, BF16),
            pltpu.VMEM((1, width), F32),
            pltpu.VMEM((1, rows), jnp.int32),
            pltpu.SemaphoreType.DMA((genes + 2,)),
        ],
        compiler_params=pltpu.CompilerParams(vmem_limit_bytes=4 * 1024 * 1024),
        name="pack",
    )(*operands)


def unpack_kernel(order, *refs):
    piece_refs, (out_hbm, sems) = refs[: len(order)], refs[len(order) :]
    gene = lax.rem(lax.axis_index("cells"), len(order))
    copies = []
    for i, (k, piece_ref) in enumerate(zip(order, piece_refs)):
        copies.append(pltpu.make_async_copy(piece_ref, out_hbm.at[gene ^ k], sems.at[i]))
        copies[-1].start()
    for copy in copies:
        copy.wait()


def unpack(pieces, order, shape):
    return pl.pallas_call(
        lambda *refs: unpack_kernel(order, *refs),
        out_shape=jax.ShapeDtypeStruct(shape, BF16),
        in_specs=[pl.BlockSpec(memory_space=pl.ANY)] * len(order),
        out_specs=pl.BlockSpec(memory_space=pltpu.HBM),
        scratch_shapes=[pltpu.SemaphoreType.DMA((len(order),))],
        compiler_params=pltpu.CompilerParams(vmem_limit_bytes=1024 * 1024),
        name="unpack",
    )(*pieces)


class Stage:
    def __init__(self, env, pieces, queries, blocks, attend, fetch=False, finish=False, keep=()):
        self.pieces, self.queries, self.blocks = pieces, queries, blocks
        self.attend, self.fetch, self.finish, self.keep = attend, fetch, finish, keep
        self.width = env["w_hbm"].shape[0]
        self.piece = env["piece"]
        self.tiles = env["adjacency_hbm"].shape[0]
        self.pairs = self.width // PAIR
        self.rows = {q: sum(size for _, _, size in pieces["q", q]) for q in {q for q, _ in attend}}
        self.cells = {b: sum(size for _, _, size in pieces["k", b]) for b in {b for _, b in attend}}
        self.block = max(self.cells.values())
        self.touched = sorted({q for q, _ in attend})
        ins = {"w_hbm", "adjacency_hbm"} if fetch else {"w"}
        if queries and not fetch:
            ins.add("adjacency")
        for group in [("q", q) for q in queries] + [("k", b) for b in {b for _, b in attend}]:
            ins |= {name for name, _, _ in pieces[group]}
        for q in self.touched:
            if q not in queries:
                ins |= {f"Q{q}", f"G{q}"}
            if f"acc{q}" in env:
                ins |= {f"acc{q}", f"top{q}"}
        for b in {b for _, b in attend} - set(blocks):
            ins |= {f"K{b}", f"V{b}"}
        if finish:
            ins.add("w_out")
        self.ins = sorted(ins)
        self.held = set(ins)
        shapes = {}
        for q in queries:
            shapes[f"Q{q}"] = ((self.pairs, 2 * self.rows[q], PAIR), BF16)
            shapes[f"G{q}"] = ((self.tiles, 2 * self.rows[q]), BF16)
        for q in self.touched:
            shapes[f"acc{q}"] = ((self.pairs, ACC_ROWS, 2 * self.rows[q]), F32)
            shapes[f"top{q}"] = ((self.pairs, 2 * self.rows[q]), F32)
        for b in blocks:
            shapes[f"K{b}"] = ((self.cells[b], self.width), BF16)
            shapes[f"V{b}"] = ((self.pairs, VAL_ROWS, self.cells[b]), BF16)
        outs, scratch = {}, {}
        for name, shape in shapes.items():
            stays = name[0] in "KV" and int(name[1:]) not in keep
            (scratch if finish or stays else outs)[name] = shape
        if finish:
            for q in self.touched:
                outs[f"out{q}"] = ((self.rows[q], self.width), BF16)
        self.outs, self.scratch = outs, scratch

    def body(self, *refs):
        count = len(self.ins)
        names = list(self.outs) + ["adjacency", "w"] * self.fetch + list(self.scratch)
        more = ["cells", "bias", "weights"] + ["attended"] * self.finish
        more += ["pairs_allowed", "sems"] * self.fetch
        self.read = dict(zip(self.ins, refs[:count]))
        self.write = dict(zip(names + more, refs[count:]))
        self.w = self.write["w"] if self.fetch else self.read["w"]
        if self.fetch:
            self.start_copies()
        if self.fetch:
            self.copies[0].wait()
        for q in self.queries:
            self.project_queries(q)
        self.late = self.fetch and len(self.attend) == 1
        if self.fetch:
            self.copies[1].wait()
            if not self.late:
                self.copies[2].wait()
        self.plan()
        self.attend_all()
        if self.finish:
            for q in self.touched:
                self.project_out(q)

    def ref(self, name):
        return self.write[name] if name in self.write else self.read[name]

    def tiles_of(self, kind, index):
        per = self.piece * self.width // LANES + ROWS
        for name, start, size in self.pieces[kind, index]:
            for piece in range(start // self.piece, (start + size) // self.piece):
                yield self.read[name], piece * per

    def start_copies(self):
        width, sems = self.width, self.write["sems"]
        moves = [(self.read["adjacency_hbm"], self.write["pairs_allowed"])]
        for start in (0, width, 2 * width):
            part = slice(start, start + width)
            moves.append((self.read["w_hbm"].at[:, part], self.write["w"].at[:, part]))
        copies = [pltpu.make_async_copy(*move, sems.at[i]) for i, move in enumerate(moves)]
        for copy in copies:
            copy.start()
        copies[0].wait()
        self.copies = copies[1:]
        allowed = self.write["pairs_allowed"][...]
        self.write["adjacency"][...] = allowed.astype(F32).astype(BF16)

    def load_cells(self, kind, index, slot=0):
        cells_ref, row = self.write["cells"].at[slot], 0
        for ref, place in self.tiles_of(kind, index):
            for _ in range(self.piece // ROWS):
                for start in range(0, self.width, LANES):
                    cells_ref[row : row + ROWS, start : start + LANES] = ref[place : place + ROWS, :]
                    place += ROWS
                row += ROWS
        return lambda: cells_ref[:row, :]

    def tags_of(self, kind, index):
        tags, parts = [], self.piece // ROWS
        for ref, place in self.tiles_of(kind, index):
            place += self.piece * self.width // LANES
            tile = ref[place : place + ROWS, :].astype(F32)
            for part in range(parts):
                column = part * (LANES // parts)
                tags.append(jnp.broadcast_to(tile[:, column : column + 1], tile.shape))
        return one_hot(jnp.concatenate(tags, axis=0), self.tiles)

    def project_queries(self, q):
        rows = self.rows[q]
        cells = self.load_cells("q", q)()
        for start in range(0, self.width, COLS):
            query = (dot(cells, self.w[:, start : start + COLS]) * SCALE).astype(BF16)
            lane = lax.broadcasted_iota(jnp.int32, (rows, PAIR), 1)
            for part in range(COLS // PAIR):
                both = query[:, part * PAIR : (part + 1) * PAIR]
                pair = start // PAIR + part
                none = jnp.zeros_like(both)
                self.write[f"Q{q}"][pair, :rows, :] = jnp.where(lane < HEAD_DIM, both, none)
                self.write[f"Q{q}"][pair, rows:, :] = jnp.where(lane < HEAD_DIM, none, both)
        near = dot(self.ref("adjacency")[...], self.tags_of("q", q), 1, 1)
        near = ((1.0 - near) * MASKED).astype(BF16)
        self.write[f"G{q}"][...] = jnp.concatenate([near, near], axis=1)

    def plan(self):
        self.due = {}
        order = [b for _, b in self.attend]
        for b in self.blocks:
            turn = order.index(b)
            cells = self.load_cells("k", b, self.blocks.index(b))
            for start in range(0, self.width, COLS):
                self.due.setdefault(turn, []).append((self.project_keys, b, cells, start))
                self.due.setdefault(turn + 1, []).append((self.project_values, b, cells, start))

    def run_due(self, turn, step=0, steps=1):
        tasks = self.due.get(turn, [])
        for task, *operands in tasks[len(tasks) * step // steps : len(tasks) * (step + 1) // steps]:
            task(*operands)

    def project_keys(self, b, cells, start):
        part = slice(self.width + start, self.width + start + COLS)
        self.write[f"K{b}"][:, start : start + COLS] = dot(cells(), self.w[:, part]).astype(BF16)

    def project_values(self, b, cells, start):
        part = slice(2 * self.width + start, 2 * self.width + start + COLS)
        values = dot(cells(), self.w[:, part]).astype(BF16).T
        for i in range(COLS // PAIR):
            pair = start // PAIR + i
            self.write[f"V{b}"][pair, :PAIR, :] = values[i * PAIR : (i + 1) * PAIR]
            ones = jnp.ones((VAL_ROWS - PAIR, self.cells[b]), BF16)
            self.write[f"V{b}"][pair, PAIR:, :] = ones

    def attend_all(self):
        source = {q: self.read for q in self.touched if f"acc{q}" in self.held}
        before = None
        self.run_due(0)
        for turn, (q, b) in enumerate(self.attend):
            after = self.start_turn(q, b, source.get(q), turn % 2)
            source[q] = self.write
            for pair in range(self.pairs):
                self.weigh(after, pair)
                if not self.late:
                    self.run_due(turn + 1, pair, self.pairs)
                if before is not None:
                    self.add_values(before, pair)
            before = after
        if self.late:
            self.copies[2].wait()
            self.run_due(len(self.attend))
        for pair in range(self.pairs):
            self.add_values(before, pair)

    def start_turn(self, q, b, before, slot):
        cells = self.cells[b]
        bias_ref = self.write["bias"].at[slot, :cells]
        bias_ref[...] = dot(self.tags_of("k", b), self.ref(f"G{q}")[...])
        return (q, b, before, bias_ref, self.write["weights"].at[slot, :, :cells], {})

    def weigh(self, turn, pair):
        q, b, before, bias_ref, weight_ref, factors = turn
        keys = self.ref(f"K{b}")[:, pair * PAIR : (pair + 1) * PAIR]
        scores = dot(keys, self.ref(f"Q{q}")[pair], 1, 1) + bias_ref[...]
        top = jnp.max(scores, axis=0, keepdims=True)
        if before is not None:
            last = before[f"top{q}"][pair : pair + 1, :]
            top = jnp.maximum(top, last)
            factors[pair] = jnp.exp2(last - top)
        else:
            top = jnp.maximum(top, LOWEST_TOP)
        weight_ref[pair] = jnp.exp2(scores - top).astype(BF16)
        self.write[f"top{q}"][pair : pair + 1, :] = top

    def add_values(self, turn, pair):
        q, b, before, _, weight_ref, factors = turn
        half = self.rows[q]
        acc_ref = self.write[f"acc{q}"]
        summed = dot(self.ref(f"V{b}")[pair], weight_ref[pair])
        even, odd = summed[:HEAD_DIM, :half], summed[HEAD_DIM:PAIR, half:]
        both = jnp.concatenate([even, odd], axis=1)
        total = summed[PAIR : PAIR + ACC_ROWS - HEAD_DIM]
        if before is not None:
            both = both + before[f"acc{q}"][pair, :HEAD_DIM, :] * factors[pair]
            total = total + before[f"acc{q}"][pair, HEAD_DIM:, :] * factors[pair]
        acc_ref[pair, :HEAD_DIM, :] = both
        acc_ref[pair, HEAD_DIM:, :] = total

    def project_out(self, q):
        half = self.rows[q]
        acc_ref, att_ref = self.write[f"acc{q}"], self.write["attended"]
        for pair in range(self.pairs):
            total = acc_ref[pair, HEAD_DIM : HEAD_DIM + 1, :]
            part = (acc_ref[pair, :HEAD_DIM, :] / total).astype(BF16)
            row = pair * PAIR
            att_ref[row : row + HEAD_DIM, :] = part[:, :half]
            att_ref[row + HEAD_DIM : row + PAIR, :] = part[:, half:]
        attended = att_ref[...].T
        for start in range(0, self.width, COLS):
            out = dot(attended, self.read["w_out"][:, start : start + COLS]).astype(BF16)
            self.write[f"out{q}"][:, start : start + COLS] = out

    def call(self, env, name):
        vmem = pl.BlockSpec(memory_space=pltpu.VMEM)
        hbm = pl.BlockSpec(memory_space=pltpu.HBM)
        operands = [env[n] for n in self.ins]
        out_shape = [jax.ShapeDtypeStruct(*shape) for shape in self.outs.values()]
        out_specs = [vmem] * len(out_shape)
        rows = max(self.rows.values())
        scratch = [pltpu.VMEM(*shape) for shape in self.scratch.values()]
        scratch += [
            pltpu.VMEM((max(len(self.blocks), 1), max(self.block, rows), self.width), BF16),
            pltpu.VMEM((2, self.block, 2 * rows), F32),
            pltpu.VMEM((2, self.pairs, self.block, 2 * rows), BF16),
        ]
        if self.finish:
            scratch.append(pltpu.VMEM((self.width, rows), BF16))
        if self.fetch:
            shape = (self.width, 3 * self.width)
            out_shape += [jax.ShapeDtypeStruct((self.tiles, self.tiles), BF16), pltpu.VMEM(shape, BF16)]
            out_specs += [vmem, vmem]
            scratch += [
                pltpu.VMEM((self.tiles, self.tiles), jnp.int32),
                pltpu.SemaphoreType.DMA((4,)),
            ]
        flops = 2 * self.width * (
            2 * sum(self.cells[b] for b in self.blocks) * self.width
            + (len(self.queries) + self.finish * len(self.touched)) * rows * self.width
            + 8 * sum(self.cells[b] for _, b in self.attend) * rows
        )
        outs = pl.pallas_call(
            self.body,
            out_shape=tuple(out_shape),
            in_specs=[hbm if n.endswith("_hbm") else vmem for n in self.ins],
            out_specs=tuple(out_specs),
            scratch_shapes=scratch,
            compiler_params=pltpu.CompilerParams(vmem_limit_bytes=16 * 1024 * 1024),
            cost_estimate=pl.CostEstimate(flops=flops, bytes_accessed=1 << 23, transcendentals=0),
            name=name,
        )(*operands)
        env.update(zip(list(self.outs) + ["adjacency", "w"] * self.fetch, outs))


def on_device(cells_in, gain, w_qkv, w_out, tile_of_cell, tile_adjacent):
    genes, cell_dev, width = cells_in.shape
    head_devs, cell_devs = lax.axis_size("heads"), lax.axis_size("cells")
    sets = cell_devs // genes
    half = genes // 2
    same = [[s * genes + g for s in range(sets)] for g in range(genes)]

    def over_cells(value, step):
        return lax.ppermute(value, "cells", [(i, i ^ step) for i in range(cell_devs)])

    def over_heads(value, step):
        return lax.ppermute(value, "heads", [(i, i ^ step) for i in range(head_devs)])

    order = [4, 1, 3, 0, 2, 6, 5, 7] if genes == 8 else list(range(genes))
    back = [0, 4, 1, 2, 6, 5, 7, 3] if genes == 8 else order
    packed = pack(cells_in, gain, tile_of_cell, order)
    arrived = [over_cells(piece, k) if k else piece for piece, k in zip(packed, order)]
    env = {"w_out": w_out, "piece": cell_dev}
    held = {"w_hbm": w_qkv, "adjacency_hbm": tile_adjacent}
    for name, value in held.items():
        env[name] = pltpu.with_memory_space_constraint(value, pltpu.HBM)
    pieces = {}
    rows = half * cell_dev

    def spread(group, own, beside):
        env[f"own{group}"] = own
        held = own
        if sets > 1:
            held = lax.all_gather(own, "cells", axis=0, axis_index_groups=same, tiled=True)
        for step in range(0, head_devs, 2):
            env[f"chunk{group}{step}"] = over_heads(held, step) if step else held
            if step in beside:
                env[f"beside{group}{step}"] = over_heads(env[f"chunk{group}{step}"], 1)

    shallow = sets == 1 and head_devs == 4
    cut = half + MORE if shallow else half
    first = jnp.concatenate(arrived[:cut], 0)
    more = (cut - half) * cell_dev
    pieces["q", 0] = [("own0", 0, rows)]
    pieces["q", 1] = [("own0", rows, more)] * (more > 0) + [("own1", 0, rows - more)]
    steps = range(0, head_devs, 2)
    spread(0, first, steps)
    if shallow:
        def env_rows(name):
            return rows + (more if "0" == name.lstrip("ownchunkbeside")[0] else -more)

        blocks = [["own0"], ["beside00", "own1"], ["beside10", "chunk02"], ["beside02", "chunk12"], ["beside12"]]
        for b, names in enumerate(blocks):
            pieces["k", b] = [(name, 0, env_rows(name)) for name in names]
        Stage(env, pieces, [0], [0], [(0, 0)], fetch=True, keep=[0]).call(env, "first_group")
        env["w"], *late = lax.optimization_barrier((env["w"], *arrived[cut:]))
        spread(1, jnp.concatenate(late, 0), [0])
        attend = [(0, 1), (1, 0), (1, 1), (0, 2), (1, 2)]
        Stage(env, pieces, [1], [1, 2], attend).call(env, "second_group")
        env["chunk12"], env["top1"] = lax.optimization_barrier((env["chunk12"], env["top1"]))
        env["beside12"] = over_heads(env["chunk12"], 1)
        Stage(env, pieces, [], [3], [(0, 3), (1, 3)]).call(env, "far")
        Stage(env, pieces, [], [4], [(0, 4), (1, 4)], finish=True).call(env, "last")
    else:
        spread(1, jnp.concatenate(arrived[half:], 0), steps)
        names = [f"{kind}{group}{step}" for group in range(2) for step in steps for kind in ("chunk", "beside")]
        for b, (name, s) in enumerate((name, s) for name in names for s in range(sets)):
            pieces["k", b] = [(name, s * rows, rows)]
        last = len(names) * sets - 1
        for b in range(last + 1):
            attend = [(0, b), (1, b)]
            stage = Stage(env, pieces, [] if b else [0, 1], [b], attend, fetch=b == 0, finish=b == last)
            stage.call(env, f"block_{b}")
    returned = []
    for k in back:
        place = order.index(k)
        start = place % half * cell_dev
        piece = env[f"out{place // half}"][start : start + cell_dev]
        returned.append(over_cells(piece, k) if k else piece)
    return unpack(returned, back, cells_in.shape)


def solution(mesh):
    return jax.shard_map(
        on_device,
        mesh=mesh,
        in_specs=(P(None, ("heads", "cells"), None), P(), P(), P(), P(("heads", "cells")), P()),
        out_specs=P(None, ("heads", "cells"), None),
        check_vma=False,
    )
```

```python
import math

import jax
import jax.numpy as jnp
from jax import lax
from jax.experimental import pallas as pl
from jax.experimental.pallas import tpu as pltpu
from jax.sharding import PartitionSpec as P

HEAD_DIM = 64
PAIR = 2 * HEAD_DIM
VAL_ROWS = PAIR + 16
ACC_ROWS = HEAD_DIM + 8
MASKED = -1e30
LOWEST_TOP = -1e29
SCALE = 0.125 * math.log2(math.e)
COLS = 256
ROWS, LANES = 16, 128
MORE = 1
BF16 = jnp.bfloat16
F32 = jnp.float32


def dot(a, b, a_dim=1, b_dim=0):
    return lax.dot_general(a, b, (((a_dim,), (b_dim,)), ((), ())), preferred_element_type=F32)


def one_hot(tags, count):
    lane = lax.broadcasted_iota(jnp.int32, tags.shape, 1).astype(F32)
    parts = [(tags == lane + start).astype(F32) for start in range(0, count, LANES)]
    return jnp.concatenate(parts, axis=1).astype(BF16)


def pack_kernel(order, x_hbm, gain_hbm, tile_hbm, *refs):
    out_refs, (cells_ref, gain_ref, tile_ref, sems) = refs[: len(order)], refs[len(order) :]
    genes, rows, width = cells_ref.shape
    gene = lax.rem(lax.axis_index("cells"), genes)
    moves = [(x_hbm.at[gene ^ k], cells_ref.at[i]) for i, k in enumerate(order)]
    moves += [(gain_hbm, gain_ref), (tile_hbm, tile_ref)]
    copies = [pltpu.make_async_copy(*move, sems.at[i]) for i, move in enumerate(moves)]
    for copy in copies:
        copy.start()
    for copy in copies:
        copy.wait()
    gain = gain_ref[...]
    row = lax.broadcasted_iota(jnp.int32, (rows, rows), 0)
    column = lax.broadcasted_iota(jnp.int32, (rows, rows), 1)
    tiles = jnp.where(row == column, tile_ref[...].astype(F32), 0.0)
    tags = jnp.sum(tiles, axis=1, keepdims=True)
    parts = rows // ROWS
    lane = lax.broadcasted_iota(jnp.int32, (ROWS, LANES), 1) // (LANES // parts)
    tag_tile = jnp.zeros((ROWS, LANES), F32)
    for part in range(parts):
        tag_tile = jnp.where(lane == part, tags[part * ROWS : (part + 1) * ROWS], tag_tile)
    for i in range(genes):
        x32 = cells_ref[i].astype(F32)
        mean = jnp.mean(x32 * x32, axis=-1, keepdims=True)
        normed = (x32 * lax.rsqrt(mean + 1e-05) * gain).astype(BF16)
        place = 0
        for row in range(0, rows, ROWS):
            for start in range(0, width, LANES):
                tile = normed[row : row + ROWS, start : start + LANES]
                out_refs[i][place : place + ROWS, :] = tile
                place += ROWS
        out_refs[i][place:, :] = tag_tile.astype(BF16)


def pack(cells_in, gain, tiles, order):
    genes, rows, width = cells_in.shape
    operands = [cells_in, gain.reshape(1, width), tiles.reshape(1, rows)]
    operands = [pltpu.with_memory_space_constraint(value, pltpu.HBM) for value in operands]
    return pl.pallas_call(
        lambda *refs: pack_kernel(order, *refs),
        out_shape=[jax.ShapeDtypeStruct((rows * width // LANES + ROWS, LANES), BF16)] * genes,
        in_specs=[pl.BlockSpec(memory_space=pltpu.HBM)] * 3,
        out_specs=[pl.BlockSpec(memory_space=pltpu.VMEM)] * genes,
        scratch_shapes=[
            pltpu.VMEM(cells_in.shape, BF16),
            pltpu.VMEM((1, width), F32),
            pltpu.VMEM((1, rows), jnp.int32),
            pltpu.SemaphoreType.DMA((genes + 2,)),
        ],
        compiler_params=pltpu.CompilerParams(vmem_limit_bytes=4 * 1024 * 1024),
        name="pack",
    )(*operands)


def unpack_kernel(order, *refs):
    piece_refs, (out_hbm, sems) = refs[: len(order)], refs[len(order) :]
    gene = lax.rem(lax.axis_index("cells"), len(order))
    copies = []
    for i, (k, piece_ref) in enumerate(zip(order, piece_refs)):
        copies.append(pltpu.make_async_copy(piece_ref, out_hbm.at[gene ^ k], sems.at[i]))
        copies[-1].start()
    for copy in copies:
        copy.wait()


def unpack(pieces, order, shape):
    return pl.pallas_call(
        lambda *refs: unpack_kernel(order, *refs),
        out_shape=jax.ShapeDtypeStruct(shape, BF16),
        in_specs=[pl.BlockSpec(memory_space=pl.ANY)] * len(order),
        out_specs=pl.BlockSpec(memory_space=pltpu.HBM),
        scratch_shapes=[pltpu.SemaphoreType.DMA((len(order),))],
        compiler_params=pltpu.CompilerParams(vmem_limit_bytes=1024 * 1024),
        name="unpack",
    )(*pieces)


class Stage:
    def __init__(self, env, pieces, queries, blocks, attend, fetch=False, finish=False, keep=()):
        self.pieces, self.queries, self.blocks = pieces, queries, blocks
        self.attend, self.fetch, self.finish, self.keep = attend, fetch, finish, keep
        self.width = env["w_hbm"].shape[0]
        self.piece = env["piece"]
        self.tiles = env["adjacency_hbm"].shape[0]
        self.pairs = self.width // PAIR
        self.rows = {q: sum(size for _, _, size in pieces["q", q]) for q in {q for q, _ in attend}}
        self.cells = {b: sum(size for _, _, size in pieces["k", b]) for b in {b for _, b in attend}}
        self.block = max(self.cells.values())
        self.touched = sorted({q for q, _ in attend})
        ins = {"w_hbm", "adjacency_hbm"} if fetch else {"w"}
        if queries and not fetch:
            ins.add("adjacency")
        for group in [("q", q) for q in queries] + [("k", b) for b in {b for _, b in attend}]:
            ins |= {name for name, _, _ in pieces[group]}
        for q in self.touched:
            if q not in queries:
                ins |= {f"Q{q}", f"G{q}"}
            if f"acc{q}" in env:
                ins |= {f"acc{q}", f"top{q}"}
        for b in {b for _, b in attend} - set(blocks):
            ins |= {f"K{b}", f"V{b}"}
        if finish:
            ins.add("w_out")
        self.ins = sorted(ins)
        self.held = set(ins)
        shapes = {}
        for q in queries:
            shapes[f"Q{q}"] = ((self.pairs, 2 * self.rows[q], PAIR), BF16)
            shapes[f"G{q}"] = ((self.tiles, 2 * self.rows[q]), BF16)
        for q in self.touched:
            shapes[f"acc{q}"] = ((self.pairs, ACC_ROWS, 2 * self.rows[q]), F32)
            shapes[f"top{q}"] = ((self.pairs, 2 * self.rows[q]), F32)
        for b in blocks:
            shapes[f"K{b}"] = ((self.cells[b], self.width), BF16)
            shapes[f"V{b}"] = ((self.pairs, VAL_ROWS, self.cells[b]), BF16)
        outs, scratch = {}, {}
        for name, shape in shapes.items():
            stays = name[0] in "KV" and int(name[1:]) not in keep
            (scratch if finish or stays else outs)[name] = shape
        if finish:
            for q in self.touched:
                outs[f"out{q}"] = ((self.rows[q], self.width), BF16)
        self.outs, self.scratch = outs, scratch

    def body(self, *refs):
        count = len(self.ins)
        names = list(self.outs) + ["adjacency", "w"] * self.fetch + list(self.scratch)
        more = ["cells", "bias", "weights"] + ["attended"] * self.finish
        more += ["pairs_allowed", "sems"] * self.fetch
        self.read = dict(zip(self.ins, refs[:count]))
        self.write = dict(zip(names + more, refs[count:]))
        self.w = self.write["w"] if self.fetch else self.read["w"]
        if self.fetch:
            self.start_copies()
        if self.fetch:
            self.copies[0].wait()
        for q in self.queries:
            self.project_queries(q)
        self.late = self.fetch and len(self.attend) == 1
        if self.fetch:
            self.copies[1].wait()
            if not self.late:
                self.copies[2].wait()
        self.plan()
        self.attend_all()
        if self.finish:
            for q in self.touched:
                self.project_out(q)

    def ref(self, name):
        return self.write[name] if name in self.write else self.read[name]

    def tiles_of(self, kind, index):
        per = self.piece * self.width // LANES + ROWS
        for name, start, size in self.pieces[kind, index]:
            for piece in range(start // self.piece, (start + size) // self.piece):
                yield self.read[name], piece * per

    def start_copies(self):
        width, sems = self.width, self.write["sems"]
        moves = [(self.read["adjacency_hbm"], self.write["pairs_allowed"])]
        for start in (0, width, 2 * width):
            part = slice(start, start + width)
            moves.append((self.read["w_hbm"].at[:, part], self.write["w"].at[:, part]))
        copies = [pltpu.make_async_copy(*move, sems.at[i]) for i, move in enumerate(moves)]
        for copy in copies:
            copy.start()
        copies[0].wait()
        self.copies = copies[1:]
        allowed = self.write["pairs_allowed"][...]
        self.write["adjacency"][...] = allowed.astype(F32).astype(BF16)

    def load_cells(self, kind, index, slot=0):
        cells_ref, row = self.write["cells"].at[slot], 0
        for ref, place in self.tiles_of(kind, index):
            for _ in range(self.piece // ROWS):
                for start in range(0, self.width, LANES):
                    cells_ref[row : row + ROWS, start : start + LANES] = ref[place : place + ROWS, :]
                    place += ROWS
                row += ROWS
        return lambda: cells_ref[:row, :]

    def tags_of(self, kind, index):
        tags, parts = [], self.piece // ROWS
        for ref, place in self.tiles_of(kind, index):
            place += self.piece * self.width // LANES
            tile = ref[place : place + ROWS, :].astype(F32)
            for part in range(parts):
                column = part * (LANES // parts)
                tags.append(jnp.broadcast_to(tile[:, column : column + 1], tile.shape))
        return one_hot(jnp.concatenate(tags, axis=0), self.tiles)

    def project_queries(self, q):
        rows = self.rows[q]
        cells = self.load_cells("q", q)()
        for start in range(0, self.width, COLS):
            query = (dot(cells, self.w[:, start : start + COLS]) * SCALE).astype(BF16)
            lane = lax.broadcasted_iota(jnp.int32, (rows, PAIR), 1)
            for part in range(COLS // PAIR):
                both = query[:, part * PAIR : (part + 1) * PAIR]
                pair = start // PAIR + part
                none = jnp.zeros_like(both)
                self.write[f"Q{q}"][pair, :rows, :] = jnp.where(lane < HEAD_DIM, both, none)
                self.write[f"Q{q}"][pair, rows:, :] = jnp.where(lane < HEAD_DIM, none, both)
        near = dot(self.ref("adjacency")[...], self.tags_of("q", q), 1, 1)
        near = ((1.0 - near) * MASKED).astype(BF16)
        self.write[f"G{q}"][...] = jnp.concatenate([near, near], axis=1)

    def plan(self):
        self.due = {}
        order = [b for _, b in self.attend]
        for b in self.blocks:
            turn = order.index(b)
            cells = self.load_cells("k", b, self.blocks.index(b))
            for start in range(0, self.width, COLS):
                self.due.setdefault(turn, []).append((self.project_keys, b, cells, start))
                self.due.setdefault(turn + 1, []).append((self.project_values, b, cells, start))

    def run_due(self, turn, step=0, steps=1):
        tasks = self.due.get(turn, [])
        for task, *operands in tasks[len(tasks) * step // steps : len(tasks) * (step + 1) // steps]:
            task(*operands)

    def project_keys(self, b, cells, start):
        part = slice(self.width + start, self.width + start + COLS)
        self.write[f"K{b}"][:, start : start + COLS] = dot(cells(), self.w[:, part]).astype(BF16)

    def project_values(self, b, cells, start):
        part = slice(2 * self.width + start, 2 * self.width + start + COLS)
        values = dot(cells(), self.w[:, part]).astype(BF16).T
        for i in range(COLS // PAIR):
            pair = start // PAIR + i
            self.write[f"V{b}"][pair, :PAIR, :] = values[i * PAIR : (i + 1) * PAIR]
            ones = jnp.ones((VAL_ROWS - PAIR, self.cells[b]), BF16)
            self.write[f"V{b}"][pair, PAIR:, :] = ones

    def attend_all(self):
        source = {q: self.read for q in self.touched if f"acc{q}" in self.held}
        before = None
        self.run_due(0)
        for turn, (q, b) in enumerate(self.attend):
            after = self.start_turn(q, b, source.get(q), turn % 2)
            source[q] = self.write
            for pair in range(self.pairs):
                self.weigh(after, pair)
                if not self.late:
                    self.run_due(turn + 1, pair, self.pairs)
                if before is not None:
                    self.add_values(before, pair)
            before = after
        if self.late:
            self.copies[2].wait()
            self.run_due(len(self.attend))
        for pair in range(self.pairs):
            self.add_values(before, pair)

    def start_turn(self, q, b, before, slot):
        cells = self.cells[b]
        bias_ref = self.write["bias"].at[slot, :cells]
        bias_ref[...] = dot(self.tags_of("k", b), self.ref(f"G{q}")[...])
        return (q, b, before, bias_ref, self.write["weights"].at[slot, :, :cells], {})

    def weigh(self, turn, pair):
        q, b, before, bias_ref, weight_ref, factors = turn
        keys = self.ref(f"K{b}")[:, pair * PAIR : (pair + 1) * PAIR]
        scores = dot(keys, self.ref(f"Q{q}")[pair], 1, 1) + bias_ref[...]
        top = jnp.max(scores, axis=0, keepdims=True)
        if before is not None:
            last = before[f"top{q}"][pair : pair + 1, :]
            top = jnp.maximum(top, last)
            factors[pair] = jnp.exp2(last - top)
        else:
            top = jnp.maximum(top, LOWEST_TOP)
        weight_ref[pair] = jnp.exp2(scores - top).astype(BF16)
        self.write[f"top{q}"][pair : pair + 1, :] = top

    def add_values(self, turn, pair):
        q, b, before, _, weight_ref, factors = turn
        half = self.rows[q]
        acc_ref = self.write[f"acc{q}"]
        summed = dot(self.ref(f"V{b}")[pair], weight_ref[pair])
        even, odd = summed[:HEAD_DIM, :half], summed[HEAD_DIM:PAIR, half:]
        both = jnp.concatenate([even, odd], axis=1)
        total = summed[PAIR : PAIR + ACC_ROWS - HEAD_DIM]
        if before is not None:
            both = both + before[f"acc{q}"][pair, :HEAD_DIM, :] * factors[pair]
            total = total + before[f"acc{q}"][pair, HEAD_DIM:, :] * factors[pair]
        acc_ref[pair, :HEAD_DIM, :] = both
        acc_ref[pair, HEAD_DIM:, :] = total

    def project_out(self, q):
        half = self.rows[q]
        acc_ref, att_ref = self.write[f"acc{q}"], self.write["attended"]
        for pair in range(self.pairs):
            total = acc_ref[pair, HEAD_DIM : HEAD_DIM + 1, :]
            part = (acc_ref[pair, :HEAD_DIM, :] / total).astype(BF16)
            row = pair * PAIR
            att_ref[row : row + HEAD_DIM, :] = part[:, :half]
            att_ref[row + HEAD_DIM : row + PAIR, :] = part[:, half:]
        attended = att_ref[...].T
        for start in range(0, self.width, COLS):
            out = dot(attended, self.read["w_out"][:, start : start + COLS]).astype(BF16)
            self.write[f"out{q}"][:, start : start + COLS] = out

    def call(self, env, name):
        vmem = pl.BlockSpec(memory_space=pltpu.VMEM)
        hbm = pl.BlockSpec(memory_space=pltpu.HBM)
        operands = [env[n] for n in self.ins]
        out_shape = [jax.ShapeDtypeStruct(*shape) for shape in self.outs.values()]
        out_specs = [vmem] * len(out_shape)
        rows = max(self.rows.values())
        scratch = [pltpu.VMEM(*shape) for shape in self.scratch.values()]
        scratch += [
            pltpu.VMEM((max(len(self.blocks), 1), max(self.block, rows), self.width), BF16),
            pltpu.VMEM((2, self.block, 2 * rows), F32),
            pltpu.VMEM((2, self.pairs, self.block, 2 * rows), BF16),
        ]
        if self.finish:
            scratch.append(pltpu.VMEM((self.width, rows), BF16))
        if self.fetch:
            shape = (self.width, 3 * self.width)
            out_shape += [jax.ShapeDtypeStruct((self.tiles, self.tiles), BF16), pltpu.VMEM(shape, BF16)]
            out_specs += [vmem, vmem]
            scratch += [
                pltpu.VMEM((self.tiles, self.tiles), jnp.int32),
                pltpu.SemaphoreType.DMA((4,)),
            ]
        flops = 2 * self.width * (
            2 * sum(self.cells[b] for b in self.blocks) * self.width
            + (len(self.queries) + self.finish * len(self.touched)) * rows * self.width
            + 8 * sum(self.cells[b] for _, b in self.attend) * rows
        )
        outs = pl.pallas_call(
            self.body,
            out_shape=tuple(out_shape),
            in_specs=[hbm if n.endswith("_hbm") else vmem for n in self.ins],
            out_specs=tuple(out_specs),
            scratch_shapes=scratch,
            compiler_params=pltpu.CompilerParams(vmem_limit_bytes=16 * 1024 * 1024),
            cost_estimate=pl.CostEstimate(flops=flops, bytes_accessed=1 << 23, transcendentals=0),
            name=name,
        )(*operands)
        env.update(zip(list(self.outs) + ["adjacency", "w"] * self.fetch, outs))


def on_device(cells_in, gain, w_qkv, w_out, tile_of_cell, tile_adjacent):
    genes, cell_dev, width = cells_in.shape
    head_devs, cell_devs = lax.axis_size("heads"), lax.axis_size("cells")
    sets = cell_devs // genes
    half = genes // 2
    same = [[s * genes + g for s in range(sets)] for g in range(genes)]

    def over_cells(value, step):
        return lax.ppermute(value, "cells", [(i, i ^ step) for i in range(cell_devs)])

    def over_heads(value, step):
        return lax.ppermute(value, "heads", [(i, i ^ step) for i in range(head_devs)])

    order = [4, 1, 3, 0, 2, 6, 5, 7] if genes == 8 else list(range(genes))
    back = [0, 4, 1, 2, 6, 5, 7, 3] if genes == 8 else order
    packed = pack(cells_in, gain, tile_of_cell, order)
    arrived = [over_cells(piece, k) if k else piece for piece, k in zip(packed, order)]
    env = {"w_out": w_out, "piece": cell_dev}
    held = {"w_hbm": w_qkv, "adjacency_hbm": tile_adjacent}
    for name, value in held.items():
        env[name] = pltpu.with_memory_space_constraint(value, pltpu.HBM)
    pieces = {}
    rows = half * cell_dev

    def spread(group, own, beside):
        env[f"own{group}"] = own
        held = own
        if sets > 1:
            held = lax.all_gather(own, "cells", axis=0, axis_index_groups=same, tiled=True)
        for step in range(0, head_devs, 2):
            env[f"chunk{group}{step}"] = over_heads(held, step) if step else held
            if step in beside:
                env[f"beside{group}{step}"] = over_heads(env[f"chunk{group}{step}"], 1)

    shallow = sets == 1 and head_devs == 4
    cut = half + MORE if shallow else half
    first = jnp.concatenate(arrived[:cut], 0)
    more = (cut - half) * cell_dev
    pieces["q", 0] = [("own0", 0, rows)]
    pieces["q", 1] = [("own0", rows, more)] * (more > 0) + [("own1", 0, rows - more)]
    steps = range(0, head_devs, 2)
    spread(0, first, steps)
    if shallow:
        def env_rows(name):
            return rows + (more if "0" == name.lstrip("ownchunkbeside")[0] else -more)

        blocks = [["own0"], ["beside00", "own1"], ["beside10", "chunk02"], ["beside02", "chunk12"], ["beside12"]]
        for b, names in enumerate(blocks):
            pieces["k", b] = [(name, 0, env_rows(name)) for name in names]
        Stage(env, pieces, [0], [0], [(0, 0)], fetch=True, keep=[0]).call(env, "first_group")
        env["w"], *late = lax.optimization_barrier((env["w"], *arrived[cut:]))
        spread(1, jnp.concatenate(late, 0), [0])
        attend = [(0, 1), (1, 0), (1, 1), (0, 2), (1, 2)]
        Stage(env, pieces, [1], [1, 2], attend).call(env, "second_group")
        env["chunk12"], env["top1"] = lax.optimization_barrier((env["chunk12"], env["top1"]))
        env["beside12"] = over_heads(env["chunk12"], 1)
        Stage(env, pieces, [], [3], [(0, 3), (1, 3)]).call(env, "far")
        Stage(env, pieces, [], [4], [(0, 4), (1, 4)], finish=True).call(env, "last")
    else:
        spread(1, jnp.concatenate(arrived[half:], 0), steps)
        names = [f"{kind}{group}{step}" for group in range(2) for step in steps for kind in ("chunk", "beside")]
        for b, (name, s) in enumerate((name, s) for name in names for s in range(sets)):
            pieces["k", b] = [(name, s * rows, rows)]
        last = len(names) * sets - 1
        for b in range(last + 1):
            attend = [(0, b), (1, b)]
            stage = Stage(env, pieces, [] if b else [0, 1], [b], attend, fetch=b == 0, finish=b == last)
            stage.call(env, f"block_{b}")
    returned = []
    for k in back:
        place = order.index(k)
        start = place % half * cell_dev
        piece = env[f"out{place // half}"][start : start + cell_dev]
        returned.append(over_cells(piece, k) if k else piece)
    return unpack(returned, back, cells_in.shape)


def solution(mesh):
    return jax.shard_map(
        on_device,
        mesh=mesh,
        in_specs=(P(None, ("heads", "cells"), None), P(), P(), P(), P(("heads", "cells")), P()),
        out_specs=P(None, ("heads", "cells"), None),
        check_vma=False,
    )
```

```python
import math

import jax
import jax.numpy as jnp
from jax import lax
from jax.experimental import pallas as pl
from jax.experimental.pallas import tpu as pltpu
from jax.sharding import PartitionSpec as P

HEAD_DIM = 64
PAIR = 2 * HEAD_DIM
VAL_ROWS = PAIR + 16
ACC_ROWS = HEAD_DIM + 8
MASKED = -1e30
LOWEST_TOP = -1e29
SCALE = 0.125 * math.log2(math.e)
COLS = 256
ROWS, LANES = 16, 128
MORE = 1
BF16 = jnp.bfloat16
F32 = jnp.float32


def dot(a, b, a_dim=1, b_dim=0):
    return lax.dot_general(a, b, (((a_dim,), (b_dim,)), ((), ())), preferred_element_type=F32)


def one_hot(tags, count):
    lane = lax.broadcasted_iota(jnp.int32, tags.shape, 1).astype(F32)
    parts = [(tags == lane + start).astype(F32) for start in range(0, count, LANES)]
    return jnp.concatenate(parts, axis=1).astype(BF16)


def pack_kernel(order, x_hbm, gain_hbm, tile_hbm, *refs):
    out_refs, (cells_ref, gain_ref, tile_ref, sems) = refs[: len(order)], refs[len(order) :]
    genes, rows, width = cells_ref.shape
    gene = lax.rem(lax.axis_index("cells"), genes)
    moves = [(x_hbm.at[gene ^ k], cells_ref.at[i]) for i, k in enumerate(order)]
    moves += [(gain_hbm, gain_ref), (tile_hbm, tile_ref)]
    copies = [pltpu.make_async_copy(*move, sems.at[i]) for i, move in enumerate(moves)]
    for copy in copies:
        copy.start()
    for copy in copies:
        copy.wait()
    gain = gain_ref[...]
    row = lax.broadcasted_iota(jnp.int32, (rows, rows), 0)
    column = lax.broadcasted_iota(jnp.int32, (rows, rows), 1)
    tiles = jnp.where(row == column, tile_ref[...].astype(F32), 0.0)
    tags = jnp.sum(tiles, axis=1, keepdims=True)
    parts = rows // ROWS
    lane = lax.broadcasted_iota(jnp.int32, (ROWS, LANES), 1) // (LANES // parts)
    tag_tile = jnp.zeros((ROWS, LANES), F32)
    for part in range(parts):
        tag_tile = jnp.where(lane == part, tags[part * ROWS : (part + 1) * ROWS], tag_tile)
    for i in range(genes):
        x32 = cells_ref[i].astype(F32)
        mean = jnp.mean(x32 * x32, axis=-1, keepdims=True)
        normed = (x32 * lax.rsqrt(mean + 1e-05) * gain).astype(BF16)
        place = 0
        for row in range(0, rows, ROWS):
            for start in range(0, width, LANES):
                tile = normed[row : row + ROWS, start : start + LANES]
                out_refs[i][place : place + ROWS, :] = tile
                place += ROWS
        out_refs[i][place:, :] = tag_tile.astype(BF16)


def pack(cells_in, gain, tiles, order):
    genes, rows, width = cells_in.shape
    operands = [cells_in, gain.reshape(1, width), tiles.reshape(1, rows)]
    operands = [pltpu.with_memory_space_constraint(value, pltpu.HBM) for value in operands]
    return pl.pallas_call(
        lambda *refs: pack_kernel(order, *refs),
        out_shape=[jax.ShapeDtypeStruct((rows * width // LANES + ROWS, LANES), BF16)] * genes,
        in_specs=[pl.BlockSpec(memory_space=pltpu.HBM)] * 3,
        out_specs=[pl.BlockSpec(memory_space=pltpu.VMEM)] * genes,
        scratch_shapes=[
            pltpu.VMEM(cells_in.shape, BF16),
            pltpu.VMEM((1, width), F32),
            pltpu.VMEM((1, rows), jnp.int32),
            pltpu.SemaphoreType.DMA((genes + 2,)),
        ],
        compiler_params=pltpu.CompilerParams(vmem_limit_bytes=4 * 1024 * 1024),
        name="pack",
    )(*operands)


def unpack_kernel(order, *refs):
    piece_refs, (out_hbm, sems) = refs[: len(order)], refs[len(order) :]
    gene = lax.rem(lax.axis_index("cells"), len(order))
    copies = []
    for i, (k, piece_ref) in enumerate(zip(order, piece_refs)):
        copies.append(pltpu.make_async_copy(piece_ref, out_hbm.at[gene ^ k], sems.at[i]))
        copies[-1].start()
    for copy in copies:
        copy.wait()


def unpack(pieces, order, shape):
    return pl.pallas_call(
        lambda *refs: unpack_kernel(order, *refs),
        out_shape=jax.ShapeDtypeStruct(shape, BF16),
        in_specs=[pl.BlockSpec(memory_space=pl.ANY)] * len(order),
        out_specs=pl.BlockSpec(memory_space=pltpu.HBM),
        scratch_shapes=[pltpu.SemaphoreType.DMA((len(order),))],
        compiler_params=pltpu.CompilerParams(vmem_limit_bytes=1024 * 1024),
        name="unpack",
    )(*pieces)


class Stage:
    def __init__(self, env, pieces, queries, blocks, attend, fetch=False, finish=False, keep=()):
        self.pieces, self.queries, self.blocks = pieces, queries, blocks
        self.attend, self.fetch, self.finish, self.keep = attend, fetch, finish, keep
        self.width = env["w_hbm"].shape[0]
        self.piece = env["piece"]
        self.tiles = env["adjacency_hbm"].shape[0]
        self.pairs = self.width // PAIR
        self.rows = {q: sum(size for _, _, size in pieces["q", q]) for q in {q for q, _ in attend}}
        self.cells = {b: sum(size for _, _, size in pieces["k", b]) for b in {b for _, b in attend}}
        self.block = max(self.cells.values())
        self.touched = sorted({q for q, _ in attend})
        ins = {"w_hbm", "adjacency_hbm"} if fetch else {"w"}
        if queries and not fetch:
            ins.add("adjacency")
        for group in [("q", q) for q in queries] + [("k", b) for b in {b for _, b in attend}]:
            ins |= {name for name, _, _ in pieces[group]}
        for q in self.touched:
            if q not in queries:
                ins |= {f"Q{q}", f"G{q}"}
            if f"acc{q}" in env:
                ins |= {f"acc{q}", f"top{q}"}
        for b in {b for _, b in attend} - set(blocks):
            ins |= {f"K{b}", f"V{b}"}
        if finish:
            ins.add("w_out")
        self.ins = sorted(ins)
        self.held = set(ins)
        shapes = {}
        for q in queries:
            shapes[f"Q{q}"] = ((self.pairs, 2 * self.rows[q], PAIR), BF16)
            shapes[f"G{q}"] = ((self.tiles, 2 * self.rows[q]), BF16)
        for q in self.touched:
            shapes[f"acc{q}"] = ((self.pairs, ACC_ROWS, 2 * self.rows[q]), F32)
            shapes[f"top{q}"] = ((self.pairs, 2 * self.rows[q]), F32)
        for b in blocks:
            shapes[f"K{b}"] = ((self.cells[b], self.width), BF16)
            shapes[f"V{b}"] = ((self.pairs, VAL_ROWS, self.cells[b]), BF16)
        outs, scratch = {}, {}
        for name, shape in shapes.items():
            stays = name[0] in "KV" and int(name[1:]) not in keep
            (scratch if finish or stays else outs)[name] = shape
        if finish:
            for q in self.touched:
                outs[f"out{q}"] = ((self.rows[q], self.width), BF16)
        self.outs, self.scratch = outs, scratch

    def body(self, *refs):
        count = len(self.ins)
        names = list(self.outs) + ["adjacency", "w"] * self.fetch + list(self.scratch)
        more = ["cells", "bias", "weights"] + ["attended"] * self.finish
        more += ["pairs_allowed", "sems"] * self.fetch
        self.read = dict(zip(self.ins, refs[:count]))
        self.write = dict(zip(names + more, refs[count:]))
        self.w = self.write["w"] if self.fetch else self.read["w"]
        if self.fetch:
            self.start_copies()
        if self.fetch:
            self.copies[0].wait()
        for q in self.queries:
            self.project_queries(q)
        self.late = self.fetch and len(self.attend) == 1
        if self.fetch:
            self.copies[1].wait()
            if not self.late:
                self.copies[2].wait()
        self.plan()
        self.attend_all()
        if self.finish:
            for q in self.touched:
                self.project_out(q)

    def ref(self, name):
        return self.write[name] if name in self.write else self.read[name]

    def tiles_of(self, kind, index):
        per = self.piece * self.width // LANES + ROWS
        for name, start, size in self.pieces[kind, index]:
            for piece in range(start // self.piece, (start + size) // self.piece):
                yield self.read[name], piece * per

    def start_copies(self):
        width, sems = self.width, self.write["sems"]
        moves = [(self.read["adjacency_hbm"], self.write["pairs_allowed"])]
        for start in (0, width, 2 * width):
            part = slice(start, start + width)
            moves.append((self.read["w_hbm"].at[:, part], self.write["w"].at[:, part]))
        copies = [pltpu.make_async_copy(*move, sems.at[i]) for i, move in enumerate(moves)]
        for copy in copies:
            copy.start()
        copies[0].wait()
        self.copies = copies[1:]
        allowed = self.write["pairs_allowed"][...]
        self.write["adjacency"][...] = allowed.astype(F32).astype(BF16)

    def load_cells(self, kind, index, slot=0):
        cells_ref, row = self.write["cells"].at[slot], 0
        for ref, place in self.tiles_of(kind, index):
            for _ in range(self.piece // ROWS):
                for start in range(0, self.width, LANES):
                    cells_ref[row : row + ROWS, start : start + LANES] = ref[place : place + ROWS, :]
                    place += ROWS
                row += ROWS
        return lambda: cells_ref[:row, :]

    def tags_of(self, kind, index):
        tags, parts = [], self.piece // ROWS
        for ref, place in self.tiles_of(kind, index):
            place += self.piece * self.width // LANES
            tile = ref[place : place + ROWS, :].astype(F32)
            for part in range(parts):
                column = part * (LANES // parts)
                tags.append(jnp.broadcast_to(tile[:, column : column + 1], tile.shape))
        return one_hot(jnp.concatenate(tags, axis=0), self.tiles)

    def project_queries(self, q):
        rows = self.rows[q]
        cells = self.load_cells("q", q)()
        for start in range(0, self.width, COLS):
            query = (dot(cells, self.w[:, start : start + COLS]) * SCALE).astype(BF16)
            lane = lax.broadcasted_iota(jnp.int32, (rows, PAIR), 1)
            for part in range(COLS // PAIR):
                both = query[:, part * PAIR : (part + 1) * PAIR]
                pair = start // PAIR + part
                none = jnp.zeros_like(both)
                self.write[f"Q{q}"][pair, :rows, :] = jnp.where(lane < HEAD_DIM, both, none)
                self.write[f"Q{q}"][pair, rows:, :] = jnp.where(lane < HEAD_DIM, none, both)
        near = dot(self.ref("adjacency")[...], self.tags_of("q", q), 1, 1)
        near = ((1.0 - near) * MASKED).astype(BF16)
        self.write[f"G{q}"][...] = jnp.concatenate([near, near], axis=1)

    def plan(self):
        self.due = {}
        order = [b for _, b in self.attend]
        for b in self.blocks:
            turn = order.index(b)
            cells = self.load_cells("k", b, self.blocks.index(b))
            for start in range(0, self.width, COLS):
                self.due.setdefault(turn, []).append((self.project_keys, b, cells, start))
                self.due.setdefault(turn + 1, []).append((self.project_values, b, cells, start))

    def run_due(self, turn, step=0, steps=1):
        tasks = self.due.get(turn, [])
        for task, *operands in tasks[len(tasks) * step // steps : len(tasks) * (step + 1) // steps]:
            task(*operands)

    def project_keys(self, b, cells, start):
        part = slice(self.width + start, self.width + start + COLS)
        self.write[f"K{b}"][:, start : start + COLS] = dot(cells(), self.w[:, part]).astype(BF16)

    def project_values(self, b, cells, start):
        part = slice(2 * self.width + start, 2 * self.width + start + COLS)
        values = dot(cells(), self.w[:, part]).astype(BF16).T
        for i in range(COLS // PAIR):
            pair = start // PAIR + i
            self.write[f"V{b}"][pair, :PAIR, :] = values[i * PAIR : (i + 1) * PAIR]
            ones = jnp.ones((VAL_ROWS - PAIR, self.cells[b]), BF16)
            self.write[f"V{b}"][pair, PAIR:, :] = ones

    def attend_all(self):
        source = {q: self.read for q in self.touched if f"acc{q}" in self.held}
        before = None
        self.run_due(0)
        for turn, (q, b) in enumerate(self.attend):
            after = self.start_turn(q, b, source.get(q), turn % 2)
            source[q] = self.write
            for pair in range(self.pairs):
                self.weigh(after, pair)
                if not self.late:
                    self.run_due(turn + 1, pair, self.pairs)
                if before is not None:
                    self.add_values(before, pair)
            before = after
        if self.late:
            self.copies[2].wait()
            self.run_due(len(self.attend))
        for pair in range(self.pairs):
            self.add_values(before, pair)

    def start_turn(self, q, b, before, slot):
        cells = self.cells[b]
        bias_ref = self.write["bias"].at[slot, :cells]
        bias_ref[...] = dot(self.tags_of("k", b), self.ref(f"G{q}")[...])
        return (q, b, before, bias_ref, self.write["weights"].at[slot, :, :cells], {})

    def weigh(self, turn, pair):
        q, b, before, bias_ref, weight_ref, factors = turn
        keys = self.ref(f"K{b}")[:, pair * PAIR : (pair + 1) * PAIR]
        scores = dot(keys, self.ref(f"Q{q}")[pair], 1, 1) + bias_ref[...]
        top = jnp.max(scores, axis=0, keepdims=True)
        if before is not None:
            last = before[f"top{q}"][pair : pair + 1, :]
            top = jnp.maximum(top, last)
            factors[pair] = jnp.exp2(last - top)
        else:
            top = jnp.maximum(top, LOWEST_TOP)
        weight_ref[pair] = jnp.exp2(scores - top).astype(BF16)
        self.write[f"top{q}"][pair : pair + 1, :] = top

    def add_values(self, turn, pair):
        q, b, before, _, weight_ref, factors = turn
        half = self.rows[q]
        acc_ref = self.write[f"acc{q}"]
        summed = dot(self.ref(f"V{b}")[pair], weight_ref[pair])
        even, odd = summed[:HEAD_DIM, :half], summed[HEAD_DIM:PAIR, half:]
        both = jnp.concatenate([even, odd], axis=1)
        total = summed[PAIR : PAIR + ACC_ROWS - HEAD_DIM]
        if before is not None:
            both = both + before[f"acc{q}"][pair, :HEAD_DIM, :] * factors[pair]
            total = total + before[f"acc{q}"][pair, HEAD_DIM:, :] * factors[pair]
        acc_ref[pair, :HEAD_DIM, :] = both
        acc_ref[pair, HEAD_DIM:, :] = total

    def project_out(self, q):
        half = self.rows[q]
        acc_ref, att_ref = self.write[f"acc{q}"], self.write["attended"]
        for pair in range(self.pairs):
            total = acc_ref[pair, HEAD_DIM : HEAD_DIM + 1, :]
            part = (acc_ref[pair, :HEAD_DIM, :] / total).astype(BF16)
            row = pair * PAIR
            att_ref[row : row + HEAD_DIM, :] = part[:, :half]
            att_ref[row + HEAD_DIM : row + PAIR, :] = part[:, half:]
        attended = att_ref[...].T
        for start in range(0, self.width, COLS):
            out = dot(attended, self.read["w_out"][:, start : start + COLS]).astype(BF16)
            self.write[f"out{q}"][:, start : start + COLS] = out

    def call(self, env, name):
        vmem = pl.BlockSpec(memory_space=pltpu.VMEM)
        hbm = pl.BlockSpec(memory_space=pltpu.HBM)
        operands = [env[n] for n in self.ins]
        out_shape = [jax.ShapeDtypeStruct(*shape) for shape in self.outs.values()]
        out_specs = [vmem] * len(out_shape)
        rows = max(self.rows.values())
        scratch = [pltpu.VMEM(*shape) for shape in self.scratch.values()]
        scratch += [
            pltpu.VMEM((max(len(self.blocks), 1), max(self.block, rows), self.width), BF16),
            pltpu.VMEM((2, self.block, 2 * rows), F32),
            pltpu.VMEM((2, self.pairs, self.block, 2 * rows), BF16),
        ]
        if self.finish:
            scratch.append(pltpu.VMEM((self.width, rows), BF16))
        if self.fetch:
            shape = (self.width, 3 * self.width)
            out_shape += [jax.ShapeDtypeStruct((self.tiles, self.tiles), BF16), pltpu.VMEM(shape, BF16)]
            out_specs += [vmem, vmem]
            scratch += [
                pltpu.VMEM((self.tiles, self.tiles), jnp.int32),
                pltpu.SemaphoreType.DMA((4,)),
            ]
        flops = 2 * self.width * (
            2 * sum(self.cells[b] for b in self.blocks) * self.width
            + (len(self.queries) + self.finish * len(self.touched)) * rows * self.width
            + 8 * sum(self.cells[b] for _, b in self.attend) * rows
        )
        outs = pl.pallas_call(
            self.body,
            out_shape=tuple(out_shape),
            in_specs=[hbm if n.endswith("_hbm") else vmem for n in self.ins],
            out_specs=tuple(out_specs),
            scratch_shapes=scratch,
            compiler_params=pltpu.CompilerParams(vmem_limit_bytes=16 * 1024 * 1024),
            cost_estimate=pl.CostEstimate(flops=flops, bytes_accessed=1 << 23, transcendentals=0),
            name=name,
        )(*operands)
        env.update(zip(list(self.outs) + ["adjacency", "w"] * self.fetch, outs))


def on_device(cells_in, gain, w_qkv, w_out, tile_of_cell, tile_adjacent):
    genes, cell_dev, width = cells_in.shape
    head_devs, cell_devs = lax.axis_size("heads"), lax.axis_size("cells")
    sets = cell_devs // genes
    half = genes // 2
    same = [[s * genes + g for s in range(sets)] for g in range(genes)]

    def over_cells(value, step):
        return lax.ppermute(value, "cells", [(i, i ^ step) for i in range(cell_devs)])

    def over_heads(value, step):
        return lax.ppermute(value, "heads", [(i, i ^ step) for i in range(head_devs)])

    order = [4, 1, 3, 2, 0, 6, 5, 7] if genes == 8 else list(range(genes))
    back = [0, 4, 1, 2, 6, 5, 7, 3] if genes == 8 else order
    packed = pack(cells_in, gain, tile_of_cell, order)
    arrived = [over_cells(piece, k) if k else piece for piece, k in zip(packed, order)]
    env = {"w_out": w_out, "piece": cell_dev}
    held = {"w_hbm": w_qkv, "adjacency_hbm": tile_adjacent}
    for name, value in held.items():
        env[name] = pltpu.with_memory_space_constraint(value, pltpu.HBM)
    pieces = {}
    rows = half * cell_dev

    def spread(group, own, beside):
        env[f"own{group}"] = own
        held = own
        if sets > 1:
            held = lax.all_gather(own, "cells", axis=0, axis_index_groups=same, tiled=True)
        for step in range(0, head_devs, 2):
            env[f"chunk{group}{step}"] = over_heads(held, step) if step else held
            if step in beside:
                env[f"beside{group}{step}"] = over_heads(env[f"chunk{group}{step}"], 1)

    shallow = sets == 1 and head_devs == 4
    cut = half + MORE if shallow else half
    first = jnp.concatenate(arrived[:cut], 0)
    more = (cut - half) * cell_dev
    pieces["q", 0] = [("own0", 0, rows)]
    pieces["q", 1] = [("own0", rows, more)] * (more > 0) + [("own1", 0, rows - more)]
    steps = range(0, head_devs, 2)
    spread(0, first, steps)
    if shallow:
        def env_rows(name):
            return rows + (more if "0" == name.lstrip("ownchunkbeside")[0] else -more)

        blocks = [["own0"], ["beside00", "own1"], ["beside10", "chunk02"], ["beside02", "chunk12"], ["beside12"]]
        for b, names in enumerate(blocks):
            pieces["k", b] = [(name, 0, env_rows(name)) for name in names]
        Stage(env, pieces, [0], [0], [(0, 0)], fetch=True, keep=[0]).call(env, "first_group")
        env["w"], *late = lax.optimization_barrier((env["w"], *arrived[cut:]))
        spread(1, jnp.concatenate(late, 0), [0])
        attend = [(0, 1), (1, 0), (1, 1), (0, 2), (1, 2)]
        Stage(env, pieces, [1], [1, 2], attend).call(env, "second_group")
        env["chunk12"], env["top1"] = lax.optimization_barrier((env["chunk12"], env["top1"]))
        env["beside12"] = over_heads(env["chunk12"], 1)
        Stage(env, pieces, [], [3], [(0, 3), (1, 3)]).call(env, "far")
        Stage(env, pieces, [], [4], [(0, 4), (1, 4)], finish=True).call(env, "last")
    else:
        spread(1, jnp.concatenate(arrived[half:], 0), steps)
        names = [f"{kind}{group}{step}" for group in range(2) for step in steps for kind in ("chunk", "beside")]
        for b, (name, s) in enumerate((name, s) for name in names for s in range(sets)):
            pieces["k", b] = [(name, s * rows, rows)]
        last = len(names) * sets - 1
        for b in range(last + 1):
            attend = [(0, b), (1, b)]
            stage = Stage(env, pieces, [] if b else [0, 1], [b], attend, fetch=b == 0, finish=b == last)
            stage.call(env, f"block_{b}")
    returned = []
    for k in back:
        place = order.index(k)
        start = place % half * cell_dev
        piece = env[f"out{place // half}"][start : start + cell_dev]
        returned.append(over_cells(piece, k) if k else piece)
    return unpack(returned, back, cells_in.shape)


def solution(mesh):
    return jax.shard_map(
        on_device,
        mesh=mesh,
        in_specs=(P(None, ("heads", "cells"), None), P(), P(), P(), P(("heads", "cells")), P()),
        out_specs=P(None, ("heads", "cells"), None),
        check_vma=False,
    )
```
